32 devices in a mesh: group: 2 (over x), span: 16 (over z, y, core).
Axes of the slice: x: 2, y: 2, z: 4, core: 2. Of those that a mesh axis runs over, the one named last changes fastest.
Arguments:
- queries: bfloat16 [8192, 2560], P(('group', 'span')), parts along dimension 0, may hold values from -6 to 6
- keys_values: bfloat16 [2, 8192, 2560], P(None, ('group', 'span')), parts along dimension 1, may hold values from -6 to 6
- owner: int32 [2], P('group'), parts along dimension 0, may hold values from 0 to 15
- span_mask: int32 [32, 3], P('group'), parts along dimension 0, may hold values 0 or 1
- lengths: int32 [32], P('group'), parts along dimension 0, may hold values from 128 to 256, as said below
- frames: bfloat16 [6, 16, 52, 384], P('group', 'span'), parts along dimension 0, may hold values from -6 to 6
- past_frames: bfloat16 [4, 16, 52, 384], P('group', 'span'), parts along dimension 0, may hold values from -5 to 5
- norm_gain: float32 [384], replicated, may hold values from 0.5 to 1.5
- conv_weight: bfloat16 [3, 3, 3, 384, 384], replicated, may hold values from -0.0625 to 0.0625
- conv_bias: float32 [384], replicated, may hold values from -3 to 3
Outputs:
- attended: bfloat16 [8192, 2560], P(('group', 'span')), parts along dimension 0
- decoded: bfloat16 [6, 16, 52, 384], P('group', 'span'), parts along dimension 0
The draws below stay inside these ranges and needn't reach their ends.
There are 2 independent parts, one for each index of `group`. The reference program is written for one: setup_inputs(seed, part) draws one part's arguments, and reference() takes and returns one part's arrays. A program takes and returns all parts, laid end to end along the dimension named above; an argument that names none is the same for every part. Nothing has to cross between parts.
Inputs may be any that keep to these rules, and one draw needn't show every extreme that they name: `lengths`: at least one slot holds exactly 256 tokens.
All inputs are finite; a program needn't handle non-finite values.
Results may differ from the reference program's by a relative error of at most 0.005.
Values may be sent and summed in bfloat16 or wider, within the bound.
A program may use at most 128 MiB of HBM per device.

```python
import jax
import jax.numpy as jnp
from jax import lax

H = 20
DH = 128
CH = 256
WIN = 4
C = 384
FRAMES = 3
PAST = 2
COLS = 52
SPANS = 16
TOKENS = 4096
ROWS = 16


def base_values(key, shape):
    return jnp.clip(1.5 * jax.random.normal(key, shape, jnp.float32), -6.0, 6.0)


def draw_queries(key, part):
    values = base_values(jax.random.fold_in(key, 1), (SPANS, CH, H * DH))
    return values.reshape(SPANS * CH, H * DH).astype(jnp.bfloat16)


def draw_keys_values(key, part):
    key_part = base_values(jax.random.fold_in(key, 2), (SPANS, CH, H * DH))
    value_part = base_values(jax.random.fold_in(key, 3), (SPANS, CH, H * DH))
    stacked = jnp.stack([key_part, value_part]).reshape(2, SPANS * CH, H * DH)
    return stacked.astype(jnp.bfloat16)


def draw_lengths(key, part):
    token_counts = jax.random.randint(jax.random.fold_in(key, 5), (SPANS,), CH // 2, CH + 1)
    longest = jax.random.randint(jax.random.fold_in(key, 6), (), 0, SPANS)
    return jnp.where(jnp.arange(SPANS) == longest, CH, token_counts).astype(jnp.int32)


def place_ends(values, stream_key, least, largest):
    extent = values.shape
    spot = [jax.random.randint(jax.random.fold_in(stream_key, axis), (), 0, extent[axis]) for axis in range(len(extent))]
    values = values.at[tuple(spot)].set(least)
    longest = extent.index(max(extent))
    spot[longest] = (spot[longest] + 1) % extent[longest]
    return values.at[tuple(spot)].set(largest)


def block_levels(key, shape, pieces, low, high):
    loudness = 1.0
    for axis_at, parts in pieces:
        draws = jax.random.uniform(jax.random.fold_in(jax.random.fold_in(key, 6), axis_at), (parts,), jnp.float32, low / len(pieces), high / len(pieces))
        loudness = loudness * jnp.repeat(jnp.exp(draws), shape[axis_at] // parts).reshape((-1,) + (1,) * (len(shape) - 1 - axis_at))
    return loudness


def normal_values(stream_key, dims, scale, bound, split=(), held_as=jnp.bfloat16):
    entries = scale * jax.random.normal(stream_key, dims, jnp.float32)
    if split:
        entries = entries * block_levels(stream_key, dims, split, -0.22, 0.18)
    return jnp.clip(entries, -bound, bound).astype(held_as)


def setup_inputs(seed: int = 0, part: int = 0) -> dict:
    streams_of = jax.random.split(jax.random.key(seed), 11)
    part_splits = jax.random.split(jax.random.fold_in(streams_of[10], part), 11)
    return {
        "queries": draw_queries(jax.random.fold_in(jax.random.fold_in(streams_of[10], part), 71), part),
        "keys_values": draw_keys_values(jax.random.fold_in(jax.random.fold_in(streams_of[10], part), 71), part),
        "owner": jax.random.randint(part_splits[2], (1,), 0, SPANS).astype(jnp.int32),
        "span_mask": place_ends((jax.random.randint(part_splits[3], (SPANS, WIN - 1), 0, 4) < 3).astype(jnp.int32), jax.random.fold_in(part_splits[3], 1), 0, 1),
        "lengths": draw_lengths(jax.random.fold_in(jax.random.fold_in(streams_of[10], part), 71), part),
        "frames": normal_values(part_splits[5], (FRAMES, ROWS, COLS, C), 1.0, 6.0, ((1, 16),)),
        "past_frames": normal_values(part_splits[6], (PAST, ROWS, COLS, C), 0.7, 5.0, ((1, 16),)),
        "norm_gain": jnp.clip(1.0 + 0.1 * jax.random.normal(streams_of[7], (C,), jnp.float32), 0.5, 1.5),
        "conv_weight": normal_values(streams_of[8], (3, 3, 3, C, C), (27 * C) ** -0.5, 0.0625),
        "conv_bias": normal_values(streams_of[9], (C,), 0.5, 3.0, (), jnp.float32),
    }


def reference(queries, keys_values, owner, span_mask, lengths, frames, past_frames, norm_gain, conv_weight, conv_bias):
    anchor = owner[0]
    row_ids = jnp.arange(CH, dtype=jnp.int32)
    score_scale = DH ** (-0.5)

    def one_span(place):
        position = (place - anchor - 1) % SPANS
        query_rows = lax.dynamic_slice_in_dim(queries, (place * CH).astype(jnp.int32), CH, 0)
        blocks = []
        valid_list = []
        for offset in range(WIN):
            source = ((place - offset) % SPANS).astype(jnp.int32)
            blocks.append(lax.dynamic_slice_in_dim(keys_values, source * CH, CH, 1))
            if offset == 0:
                allowed = jnp.array(True)
            else:
                allowed = (position >= offset) & (span_mask[position, offset - 1] == 1)
            valid_list.append(allowed & (row_ids < lengths[source]))
        blocks.append(lax.dynamic_slice_in_dim(keys_values, (anchor * CH).astype(jnp.int32), CH, 1))
        valid_list.append((place != anchor) & (row_ids < lengths[anchor]))
        gathered = jnp.concatenate(blocks, axis=1)
        key_valid = jnp.concatenate(valid_list)
        query_heads = query_rows.reshape(CH, H, DH).astype(jnp.float32)
        key_heads = gathered[0].reshape(-1, H, DH).astype(jnp.float32)
        value_heads = gathered[1].reshape(-1, H, DH).astype(jnp.float32)
        scores = jnp.einsum('qhd,khd->hqk', query_heads, key_heads) * score_scale
        scores = jnp.where(key_valid[None, None, :], scores, -jnp.inf)
        row_max = lax.optimization_barrier(jnp.max(scores, axis=-1, keepdims=True))
        weights = jnp.exp(scores - row_max)
        probs = (weights / lax.optimization_barrier(jnp.sum(weights, axis=-1, keepdims=True))).astype(jnp.bfloat16)
        blended = jnp.einsum('hqk,khd->qhd', probs.astype(jnp.float32), value_heads).reshape(CH, H * DH)
        blended = jnp.where(row_ids[:, None] < lengths[place], blended, 0.0)
        return blended.astype(jnp.bfloat16)
    attended = lax.map(one_span, jnp.arange(SPANS, dtype=jnp.int32)).reshape(TOKENS, H * DH)
    features = frames.astype(jnp.float32)
    squares = lax.optimization_barrier(jnp.mean(features * features, axis=-1, keepdims=True))
    normed = features * lax.rsqrt(squares + 1e-06) * norm_gain
    activated = jax.nn.silu(normed).astype(jnp.bfloat16)
    stacked = jnp.concatenate([past_frames, activated], axis=0)
    padded = jnp.pad(stacked, ((0, 0), (1, 1), (1, 1), (0, 0)))
    windows = []
    for frame_tap in range(3):
        for row_tap in range(3):
            for col_tap in range(3):
                windows.append(padded[frame_tap:frame_tap + FRAMES, row_tap:row_tap + ROWS, col_tap:col_tap + COLS, :])
    columns = jnp.concatenate(windows, axis=-1).reshape(-1, 27 * C)
    convolved = jnp.dot(columns, conv_weight.reshape(27 * C, C), preferred_element_type=jnp.float32)
    decoded = features + conv_bias + convolved.reshape(FRAMES, ROWS, COLS, C)
    return (attended, decoded.astype(jnp.bfloat16))
```

```python
import functools

import jax
import jax.numpy as jnp
from jax import lax
from jax.experimental import pallas as pl
from jax.experimental.pallas import tpu as pltpu
from jax.sharding import PartitionSpec as P

DH = 128
WIN = 4
PIECES = 10
AHEAD = 4
LOG2E = 1.4426950408889634
MESH = pl.DeviceIdType.MESH


def attention_kernel(
    n, owner_ref, q_ref, kv_ref, bias_ref, out_ref, slots, up_in, down_in, up_out, down_out, recv, send
):
    rows = n // 4
    width = q_ref.shape[1] // PIECES
    me = lax.axis_index("span")
    role = lax.rem(me, 4)
    z = me // 4

    def at(offset):
        return lax.rem(me + offset + n, n)

    def columns(piece):
        return pl.ds(pl.multiple_of(piece * width, width), width)

    def own(piece):
        return kv_ref.at[:, :, columns(piece)]

    def to_slot(source, slot, piece, lane, offset):
        return pltpu.make_async_remote_copy(
            src_ref=source,
            dst_ref=slots.at[slot, piece],
            send_sem=send.at[lane, piece],
            recv_sem=recv.at[slot, piece],
            device_id={"span": at(offset)},
            device_id_type=MESH,
        )

    def wave(source, target, kind, piece, offset):
        return pltpu.make_async_remote_copy(
            src_ref=source.at[piece],
            dst_ref=target.at[piece],
            send_sem=send.at[kind, piece],
            recv_sem=recv.at[kind, piece],
            device_id={"span": at(offset)},
            device_id_type=MESH,
        )

    def arrived(slot, piece):
        to_slot(slots.at[slot, piece], slot, piece, 0, 1).wait_recv()

    barrier = pltpu.get_barrier_semaphore()
    for offset in (-4, -3, -2, -1, 1, 2, 3, 4):
        pl.semaphore_signal(barrier, inc=1, device_id={"span": at(offset)}, device_id_type=MESH)
    pl.semaphore_wait(barrier, 8)

    direct = {
        0: ((1, 1, 2), (0, 0, 1)),
        1: ((2, 0, 3), (1, 1, 2)),
        2: ((1, 1, 2), (0, 0, 1)),
        3: ((2, 0, 3),),
    }

    def send_own(piece):
        for which, copies in direct.items():

            @pl.when(role == which)
            def _():
                for slot, lane, offset in copies:
                    to_slot(own(piece), slot, piece, lane, offset).start()

    passed = {
        0: ((1, 2, 2, 1), (0, 1, 3, 1)),
        2: ((2, 0, 2, -2), (1, 2, 3, 1)),
        3: ((1, 0, 2, -1),),
    }
    kept = {0: (2,), 1: (0, 1, 2), 2: (0,), 3: (0, 2)}

    def window(piece):
        for which in range(4):

            @pl.when(role == which)
            def _():
                for slot, there, lane, offset in passed.get(which, ()):
                    arrived(slot, piece)
                    to_slot(slots.at[slot, piece], there, piece, lane, offset).start()
                for slot in kept[which]:
                    arrived(slot, piece)

    anchor = owner_ref[0]
    behind = lax.rem(me - anchor + n, n)
    group = jnp.where(role == 0, lax.rem((anchor + 3) // 4, rows), anchor // 4)

    def mine(piece, part):
        value = jnp.where(behind == 2, slots[1, piece, part], slots[2, piece, part])
        value = jnp.where(behind == 1, slots[0, piece, part], value)
        return jnp.where(behind == 0, kv_ref[part, :, columns(piece)], value)

    def crosses(piece):
        return lax.rem(piece, 2) == 1

    def waves(piece):
        return (role == 3) | ((role == 0) & jnp.logical_not(crosses(piece)))

    def within(piece):
        return (piece >= 0) & (piece < PIECES)

    def attend(piece):
        for sub in range(width // DH):
            cols = pl.ds(pl.multiple_of(piece * width + sub * DH, DH), DH)
            inner = slice(sub * DH, (sub + 1) * DH)
            query = q_ref[:, cols]
            scores = []
            for block in range(5):
                key = kv_ref[0, :, cols] if block == 0 else slots[block - 1, piece, 0, :, inner]
                score = lax.dot_general(
                    query, key, (((1,), (1,)), ((), ())), preferred_element_type=jnp.float32
                )
                scores.append(score * (DH**-0.5 * LOG2E) + bias_ref[block : block + 1, :])
            top = functools.reduce(jnp.maximum, scores)
            top = jnp.max(top, axis=-1, keepdims=True)
            weights = [jnp.exp2(score - top) for score in scores]
            total = jnp.sum(functools.reduce(jnp.add, weights), axis=-1, keepdims=True)
            blended = None
            for block in range(5):
                value = kv_ref[1, :, cols] if block == 0 else slots[block - 1, piece, 1, :, inner]
                term = jnp.dot(
                    weights[block].astype(jnp.bfloat16), value, preferred_element_type=jnp.float32
                )
                blended = term if blended is None else blended + term
            out_ref[:, cols] = (blended / total).astype(out_ref.dtype)

    def start(piece, _):
        send_own(piece)
        return 0

    lax.fori_loop(0, AHEAD, start, 0)

    def step(t, _):
        @pl.when(t + AHEAD < PIECES)
        def _():
            send_own(t + AHEAD)

        @pl.when(t < PIECES)
        def _():
            window(t)

        rising = t - z
        falling = t - (rows - 1 - z)
        final = t - (rows - 1)
        ready = t - rows

        @pl.when(within(rising) & waves(rising))
        def _():
            @pl.when(z > 0)
            def _():
                wave(up_out, up_in, 4, rising, 4).wait_recv()

            @pl.when(z < rows - 1)
            def _():
                for part in range(2):
                    up_out[rising, part] = jnp.where(
                        group == z, mine(rising, part), up_in[rising, part]
                    )
                wave(up_out, up_in, 4, rising, 4).start()

        @pl.when(within(falling) & waves(falling))
        def _():
            @pl.when(z < rows - 1)
            def _():
                wave(down_out, down_in, 5, falling, -4).wait_recv()

            @pl.when(z > 0)
            def _():
                for part in range(2):
                    down_out[falling, part] = jnp.where(
                        group == z, mine(falling, part), down_in[falling, part]
                    )
                wave(down_out, down_in, 5, falling, -4).start()

        @pl.when(within(final) & waves(final))
        def _():
            for part in range(2):
                value = jnp.where(group < z, up_in[final, part], down_in[final, part])
                slots[3, final, part] = jnp.where(group == z, mine(final, part), value)

            @pl.when((role == 3) & crosses(final))
            def _():
                to_slot(slots.at[3, final], 3, final, 7, -3).start()

            @pl.when(role == 3)
            def _():
                to_slot(slots.at[3, final], 3, final, 6, -1).start()

            @pl.when(role == 0)
            def _():
                to_slot(slots.at[3, final], 3, final, 6, 1).start()

        @pl.when(within(ready))
        def _():
            @pl.when((role == 0) & crosses(ready))
            def _():
                arrived(3, ready)
                to_slot(slots.at[3, ready], 3, ready, 6, 1).start()

            @pl.when((role == 1) | (role == 2))
            def _():
                arrived(3, ready)

            attend(ready)

        return 0

    lax.fori_loop(0, PIECES + rows, step, 0)

    def finish(piece, _):
        for which in range(4):

            @pl.when(role == which)
            def _():
                for slot, lane, offset in direct[which]:
                    to_slot(own(piece), slot, piece, lane, offset).wait_send()
                for slot, there, lane, offset in passed.get(which, ()):
                    to_slot(slots.at[slot, piece], there, piece, lane, offset).wait_send()

        @pl.when(waves(piece) & (z < rows - 1))
        def _():
            wave(up_out, up_in, 4, piece, 4).wait_send()

        @pl.when(waves(piece) & (z > 0))
        def _():
            wave(down_out, down_in, 5, piece, -4).wait_send()

        @pl.when((role == 0) | (role == 3))
        def _():
            to_slot(slots.at[3, piece], 3, piece, 6, 1).wait_send()

        @pl.when((role == 3) & crosses(piece))
        def _():
            to_slot(slots.at[3, piece], 3, piece, 7, -3).wait_send()

        return 0

    lax.fori_loop(0, PIECES, finish, 0)


def attention(queries, keys_values, owner, bias):
    n = lax.axis_size("span")
    rows, cols = queries.shape
    piece = (PIECES, 2, rows, cols // PIECES)
    flops = 4 * rows * 5 * rows * cols
    return pl.pallas_call(
        functools.partial(attention_kernel, n),
        out_shape=jax.ShapeDtypeStruct((rows, cols), jnp.bfloat16),
        in_specs=[pl.BlockSpec(memory_space=pltpu.SMEM)] + [pl.BlockSpec(memory_space=pltpu.VMEM)] * 3,
        out_specs=pl.BlockSpec(memory_space=pltpu.VMEM),
        scratch_shapes=[
            pltpu.VMEM((4,) + piece, jnp.bfloat16),
            pltpu.VMEM(piece, jnp.bfloat16),
            pltpu.VMEM(piece, jnp.bfloat16),
            pltpu.VMEM(piece, jnp.bfloat16),
            pltpu.VMEM(piece, jnp.bfloat16),
            pltpu.SemaphoreType.DMA((6, PIECES)),
            pltpu.SemaphoreType.DMA((8, PIECES)),
        ],
        cost_estimate=pl.CostEstimate(
            flops=flops, bytes_accessed=8 * rows * cols, transcendentals=5 * rows * rows * cols // DH
        ),
        compiler_params=pltpu.CompilerParams(
            collective_id=0, has_side_effects=True, vmem_limit_bytes=52 * 1024 * 1024
        ),
        name="span_attention",
    )(owner, queries, keys_values, bias)


def extended_2(block, sides, width):
    for axis, dim in sides:
        count = lax.axis_size(axis)
        forward = [(i, i + 1) for i in range(count - 1)]
        backward = [(target, source) for source, target in forward]
        low = lax.ppermute(
            lax.slice_in_dim(block, block.shape[dim] - width, None, axis=dim), axis, forward
        )
        high = lax.ppermute(lax.slice_in_dim(block, 0, width, axis=dim), axis, backward)
        block = jnp.concatenate([low, block, high], axis=dim)
    return block


def shards(
    queries,
    keys_values,
    owner,
    span_mask,
    lengths,
    frames,
    past_frames,
    norm_gain,
    conv_weight,
    conv_bias,
):
    devices = lax.axis_size("span")
    place = lax.axis_index("span")
    anchor = owner[0]
    position = (place - anchor - 1) % devices
    tok_rows = queries.shape[0]
    row_ids = jnp.arange(tok_rows, dtype=jnp.int32)
    valid_list = [row_ids < lengths[place]]
    for offset in range(1, WIN):
        source = (place - offset) % devices
        allowed = (position >= offset) & (span_mask[position, offset - 1] == 1)
        valid_list.append(allowed & (row_ids < lengths[source]))
    valid_list.append((place != anchor) & (row_ids < lengths[anchor]))
    bias = jnp.where(jnp.stack(valid_list), 0.0, -1e30).astype(jnp.float32)
    bias = jnp.pad(bias, ((0, 3), (0, 0)))
    attended = attention(queries, keys_values, owner, bias)
    attended = jnp.where(row_ids[:, None] < lengths[place], attended, 0.0).astype(jnp.bfloat16)
    features = frames.astype(jnp.float32)
    squares = jnp.mean(features * features, axis=-1, keepdims=True)
    normed = features * lax.rsqrt(squares + 1e-06) * norm_gain
    activated = jax.nn.silu(normed).astype(jnp.bfloat16)
    stacked = jnp.concatenate([past_frames, activated], axis=0)
    extended = extended_2(stacked, (("span", 1),), 1)
    padded = jnp.pad(extended, ((0, 0), (0, 0), (1, 1), (0, 0)))
    frame_count = frames.shape[0]
    rows_here = frames.shape[1]
    col_count = frames.shape[2]
    channels = frames.shape[3]
    windows = []
    for frame_tap in range(3):
        for row_tap in range(3):
            for col_tap in range(3):
                windows.append(
                    padded[
                        frame_tap : frame_tap + frame_count,
                        row_tap : row_tap + rows_here,
                        col_tap : col_tap + col_count,
                        :,
                    ]
                )
    columns = jnp.concatenate(windows, axis=-1).reshape(-1, 27 * channels)
    convolved = jnp.dot(
        columns, conv_weight.reshape(27 * channels, channels), preferred_element_type=jnp.float32
    )
    decoded = features + conv_bias + convolved.reshape(frame_count, rows_here, col_count, channels)
    return (attended, decoded.astype(jnp.bfloat16))


def solution(mesh):
    placed = (
        P(("group", "span"), None),
        P(None, ("group", "span"), None),
        P("group"),
        P("group", None),
        P("group"),
        P("group", "span", None, None),
        P("group", "span", None, None),
        P(),
        P(),
        P(),
    )
    return jax.shard_map(
        shards,
        mesh=mesh,
        in_specs=placed,
        out_specs=(P(("group", "span"), None), P("group", "span", None, None)),
        check_vma=False,
    )
```

```python
import functools

import jax
import jax.numpy as jnp
from jax import lax
from jax.experimental import pallas as pl
from jax.experimental.pallas import tpu as pltpu
from jax.sharding import PartitionSpec as P

DH = 128
WIN = 4
PIECES = 10
AHEAD = 4
LOG2E = 1.4426950408889634
MESH = pl.DeviceIdType.MESH


def block_kernel(
    n,
    owner_ref,
    mask_ref,
    lengths_ref,
    q_ref,
    kv_ref,
    frames_ref,
    past_ref,
    gain_ref,
    shift_ref,
    weight_ref,
    out_ref,
    decoded_ref,
    slots,
    up_in,
    down_in,
    up_out,
    down_out,
    taps,
    weights_here,
    partial,
    recv,
    send,
    edge_recv,
    edge_send,
    weight_sem,
):
    tokens = q_ref.shape[0]
    frames, _, cols, channels = frames_ref.shape
    past = past_ref.shape[0]
    padded = taps.shape[2]
    rows = n // 4
    width = q_ref.shape[1] // PIECES
    me = lax.axis_index("span")
    role = lax.rem(me, 4)
    z = me // 4

    def at(offset):
        return lax.rem(me + offset + n, n)

    def columns(piece):
        return pl.ds(pl.multiple_of(piece * width, width), width)

    def own(piece):
        return kv_ref.at[:, :, columns(piece)]

    def to_slot(source, slot, piece, lane, offset):
        return pltpu.make_async_remote_copy(
            src_ref=source,
            dst_ref=slots.at[slot, piece],
            send_sem=send.at[lane, piece],
            recv_sem=recv.at[slot, piece],
            device_id={"span": at(offset)},
            device_id_type=MESH,
        )

    def wave(source, target, kind, piece, offset):
        return pltpu.make_async_remote_copy(
            src_ref=source.at[piece],
            dst_ref=target.at[piece],
            send_sem=send.at[kind, piece],
            recv_sem=recv.at[kind, piece],
            device_id={"span": at(offset)},
            device_id_type=MESH,
        )

    def arrived(slot, piece):
        to_slot(slots.at[slot, piece], slot, piece, 0, 1).wait_recv()

    def edge(which):
        return pltpu.make_async_remote_copy(
            src_ref=taps.at[1],
            dst_ref=taps.at[2 * which],
            send_sem=edge_send.at[which],
            recv_sem=edge_recv.at[which],
            device_id={"span": at(1 - 2 * which)},
            device_id_type=MESH,
        )

    weight_copy = pltpu.make_async_copy(weight_ref, weights_here, weight_sem)
    weight_copy.start()

    barrier = pltpu.get_barrier_semaphore()
    for offset in (-4, -3, -2, -1, 1, 2, 3, 4):
        pl.semaphore_signal(barrier, inc=1, device_id={"span": at(offset)}, device_id_type=MESH)
    pl.semaphore_wait(barrier, 8)

    direct = {
        0: ((1, 1, 2), (0, 0, 1)),
        1: ((2, 0, 3), (1, 1, 2)),
        2: ((1, 1, 2), (0, 0, 1)),
        3: ((2, 0, 3),),
    }

    def send_own(piece):
        for which, copies in direct.items():

            @pl.when(role == which)
            def _():
                for slot, lane, offset in copies:
                    to_slot(own(piece), slot, piece, lane, offset).start()

    passed = {
        0: ((1, 2, 2, 1), (0, 1, 3, 1)),
        2: ((2, 0, 2, -2), (1, 2, 3, 1)),
        3: ((1, 0, 2, -1),),
    }
    kept = {0: (2,), 1: (0, 1, 2), 2: (0,), 3: (0, 2)}

    def window(piece):
        for which in range(4):

            @pl.when(role == which)
            def _():
                for slot, there, lane, offset in passed.get(which, ()):
                    arrived(slot, piece)
                    to_slot(slots.at[slot, piece], there, piece, lane, offset).start()
                for slot in kept[which]:
                    arrived(slot, piece)

    anchor = owner_ref[0]
    behind = lax.rem(me - anchor + n, n)
    group = jnp.where(role == 0, lax.rem((anchor + 3) // 4, rows), anchor // 4)

    def mine(piece, part):
        value = jnp.where(behind == 2, slots[1, piece, part], slots[2, piece, part])
        value = jnp.where(behind == 1, slots[0, piece, part], value)
        return jnp.where(behind == 0, kv_ref[part, :, columns(piece)], value)

    def crosses(piece):
        return lax.rem(piece, 2) == 1

    def waves(piece):
        return (role == 3) | ((role == 0) & jnp.logical_not(crosses(piece)))

    def within(piece):
        return (piece >= 0) & (piece < PIECES)

    position = lax.rem(me - anchor - 1 + 2 * n, n)
    length = lengths_ref[me]
    limits = [length]
    for offset in range(1, WIN):
        allowed = (position >= offset) & (mask_ref[position, offset - 1] == 1)
        limits.append(jnp.where(allowed, lengths_ref[at(-offset)], 0))
    limits.append(jnp.where(behind == 0, 0, lengths_ref[anchor]))

    def activate():
        spare = partial.at[0, 0, 0:padded, :]
        for frame in range(past + frames):
            if frame < past:
                value = past_ref[frame, 0].astype(jnp.float32)
            else:
                value = frames_ref[frame - past, 0].astype(jnp.float32)
                squares = jnp.mean(value * value, axis=-1, keepdims=True)
                value = value * lax.rsqrt(squares + 1e-06) * gain_ref[...]
                value = value / (1.0 + jnp.exp(-value))
            spare[...] = jnp.zeros(spare.shape, jnp.float32)
            spare[0:cols, :] = value
            taps[1, frame] = spare[...].astype(jnp.bfloat16)
        partial[0, :, 0:8, :] = jnp.zeros((frames, 8, channels), jnp.float32)

        @pl.when(me < n - 1)
        def _():
            edge(0).start()

        @pl.when(me > 0)
        def _():
            edge(1).start()

        @pl.when(me == 0)
        def _():
            taps[0] = jnp.zeros(taps.shape[1:], taps.dtype)

        @pl.when(me == n - 1)
        def _():
            taps[2] = jnp.zeros(taps.shape[1:], taps.dtype)

    def edges_arrived():
        @pl.when(me > 0)
        def _():
            edge(0).wait_recv()

        @pl.when(me < n - 1)
        def _():
            edge(1).wait_recv()

        weight_copy.wait()

    def convolve(col_tap):
        total = None
        for frame_tap in range(3):
            for row_tap in range(3):
                window_rows = taps[row_tap, frame_tap : frame_tap + frames]
                term = jnp.dot(
                    window_rows.reshape(frames * padded, channels),
                    weights_here[frame_tap, row_tap, col_tap],
                    preferred_element_type=jnp.float32,
                )
                total = term if total is None else total + term
        partial[col_tap, :, 8 : 8 + padded, :] = total.reshape(frames, padded, channels)

    def decode():
        for frame in range(frames):
            total = frames_ref[frame, 0].astype(jnp.float32) + shift_ref[...]
            for col_tap in range(3):
                total = total + partial[col_tap, frame, 7 + col_tap : 7 + col_tap + cols, :]
            decoded_ref[frame, 0] = total.astype(decoded_ref.dtype)

    def attend(piece):
        token = lax.broadcasted_iota(jnp.int32, (1, tokens), 1)
        hidden = [jnp.where(token < limit, 0.0, -1e30) for limit in limits]
        row = lax.broadcasted_iota(jnp.int32, (tokens, 1), 0)
        for sub in range(width // DH):
            cols = pl.ds(pl.multiple_of(piece * width + sub * DH, DH), DH)
            inner = slice(sub * DH, (sub + 1) * DH)
            query = q_ref[:, cols]
            scores = []
            for block in range(5):
                key = kv_ref[0, :, cols] if block == 0 else slots[block - 1, piece, 0, :, inner]
                score = lax.dot_general(
                    query, key, (((1,), (1,)), ((), ())), preferred_element_type=jnp.float32
                )
                scores.append(score * (DH**-0.5 * LOG2E) + hidden[block])
            top = functools.reduce(jnp.maximum, scores)
            top = jnp.max(top, axis=-1, keepdims=True)
            weights = [jnp.exp2(score - top) for score in scores]
            total = jnp.sum(functools.reduce(jnp.add, weights), axis=-1, keepdims=True)
            blended = None
            for block in range(5):
                value = kv_ref[1, :, cols] if block == 0 else slots[block - 1, piece, 1, :, inner]
                term = jnp.dot(
                    weights[block].astype(jnp.bfloat16), value, preferred_element_type=jnp.float32
                )
                blended = term if blended is None else blended + term
            out_ref[:, cols] = jnp.where(row < length, blended / total, 0.0).astype(out_ref.dtype)

    def start(piece, _):
        send_own(piece)
        return 0

    lax.fori_loop(0, AHEAD, start, 0)
    activate()

    def step(t, _):
        @pl.when(t + AHEAD < PIECES)
        def _():
            send_own(t + AHEAD)

        @pl.when(t < PIECES)
        def _():
            window(t)

        @pl.when(t == 2)
        def _():
            edges_arrived()

        @pl.when((t >= 2) & (t < 5))
        def _():
            convolve(t - 2)

        @pl.when(t == 5)
        def _():
            decode()

        rising = t - z
        falling = t - (rows - 1 - z)
        final = t - (rows - 1)
        ready = t - rows

        @pl.when(within(rising) & waves(rising))
        def _():
            @pl.when(z > 0)
            def _():
                wave(up_out, up_in, 4, rising, 4).wait_recv()

            @pl.when(z < rows - 1)
            def _():
                for part in range(2):
                    up_out[rising, part] = jnp.where(
                        group == z, mine(rising, part), up_in[rising, part]
                    )
                wave(up_out, up_in, 4, rising, 4).start()

        @pl.when(within(falling) & waves(falling))
        def _():
            @pl.when(z < rows - 1)
            def _():
                wave(down_out, down_in, 5, falling, -4).wait_recv()

            @pl.when(z > 0)
            def _():
                for part in range(2):
                    down_out[falling, part] = jnp.where(
                        group == z, mine(falling, part), down_in[falling, part]
                    )
                wave(down_out, down_in, 5, falling, -4).start()

        @pl.when(within(final) & waves(final))
        def _():
            for part in range(2):
                value = jnp.where(group < z, up_in[final, part], down_in[final, part])
                slots[3, final, part] = jnp.where(group == z, mine(final, part), value)

            @pl.when((role == 3) & crosses(final))
            def _():
                to_slot(slots.at[3, final], 3, final, 7, -3).start()

            @pl.when(role == 3)
            def _():
                to_slot(slots.at[3, final], 3, final, 6, -1).start()

            @pl.when(role == 0)
            def _():
                to_slot(slots.at[3, final], 3, final, 6, 1).start()

        @pl.when(within(ready))
        def _():
            @pl.when((role == 0) & crosses(ready))
            def _():
                arrived(3, ready)
                to_slot(slots.at[3, ready], 3, ready, 6, 1).start()

            @pl.when((role == 1) | (role == 2))
            def _():
                arrived(3, ready)

            attend(ready)

        return 0

    lax.fori_loop(0, PIECES + rows, step, 0)

    def finish(piece, _):
        for which in range(4):

            @pl.when(role == which)
            def _():
                for slot, lane, offset in direct[which]:
                    to_slot(own(piece), slot, piece, lane, offset).wait_send()
                for slot, there, lane, offset in passed.get(which, ()):
                    to_slot(slots.at[slot, piece], there, piece, lane, offset).wait_send()

        @pl.when(waves(piece) & (z < rows - 1))
        def _():
            wave(up_out, up_in, 4, piece, 4).wait_send()

        @pl.when(waves(piece) & (z > 0))
        def _():
            wave(down_out, down_in, 5, piece, -4).wait_send()

        @pl.when((role == 0) | (role == 3))
        def _():
            to_slot(slots.at[3, piece], 3, piece, 6, 1).wait_send()

        @pl.when((role == 3) & crosses(piece))
        def _():
            to_slot(slots.at[3, piece], 3, piece, 7, -3).wait_send()

        return 0

    lax.fori_loop(0, PIECES, finish, 0)

    @pl.when(me < n - 1)
    def _():
        edge(0).wait_send()

    @pl.when(me > 0)
    def _():
        edge(1).wait_send()


def shards(
    queries,
    keys_values,
    owner,
    span_mask,
    lengths,
    frames,
    past_frames,
    norm_gain,
    conv_weight,
    conv_bias,
):
    n = lax.axis_size("span")
    rows, cols = queries.shape
    piece = (PIECES, 2, rows, cols // PIECES)
    frame_count, _, frame_cols, channels = frames.shape
    padded = -(-(frame_cols + 1) // 16) * 16
    attention_flops = 4 * rows * 5 * rows * cols
    conv_flops = 2 * frame_count * frame_cols * conv_weight.size
    scalars = pl.BlockSpec(memory_space=pltpu.SMEM)
    whole = pl.BlockSpec(memory_space=pltpu.VMEM)
    return pl.pallas_call(
        functools.partial(block_kernel, n),
        out_shape=(
            jax.ShapeDtypeStruct((rows, cols), jnp.bfloat16),
            jax.ShapeDtypeStruct(frames.shape, jnp.bfloat16),
        ),
        in_specs=[scalars] * 3 + [whole] * 6 + [pl.BlockSpec(memory_space=pl.ANY)],
        out_specs=(whole, whole),
        scratch_shapes=[
            pltpu.VMEM((4,) + piece, jnp.bfloat16),
            pltpu.VMEM(piece, jnp.bfloat16),
            pltpu.VMEM(piece, jnp.bfloat16),
            pltpu.VMEM(piece, jnp.bfloat16),
            pltpu.VMEM(piece, jnp.bfloat16),
            pltpu.VMEM((3, frame_count + past_frames.shape[0], padded, channels), jnp.bfloat16),
            pltpu.VMEM(conv_weight.shape, jnp.bfloat16),
            pltpu.VMEM((3, frame_count, padded + 16, channels), jnp.float32),
            pltpu.SemaphoreType.DMA((6, PIECES)),
            pltpu.SemaphoreType.DMA((8, PIECES)),
            pltpu.SemaphoreType.DMA((2,)),
            pltpu.SemaphoreType.DMA((2,)),
            pltpu.SemaphoreType.DMA,
        ],
        cost_estimate=pl.CostEstimate(
            flops=attention_flops + conv_flops,
            bytes_accessed=8 * rows * cols + 2 * conv_weight.size,
            transcendentals=5 * rows * rows * cols // DH,
        ),
        compiler_params=pltpu.CompilerParams(
            collective_id=0, has_side_effects=True, vmem_limit_bytes=60 * 1024 * 1024
        ),
        name="spans_and_decoder",
    )(
        owner,
        span_mask,
        lengths,
        queries,
        keys_values,
        frames,
        past_frames,
        norm_gain.reshape(1, channels),
        conv_bias.reshape(1, channels),
        conv_weight,
    )


def solution(mesh):
    placed = (
        P(("group", "span"), None),
        P(None, ("group", "span"), None),
        P("group"),
        P("group", None),
        P("group"),
        P("group", "span", None, None),
        P("group", "span", None, None),
        P(),
        P(),
        P(),
    )
    return jax.shard_map(
        shards,
        mesh=mesh,
        in_specs=placed,
        out_specs=(P(("group", "span"), None), P("group", "span", None, None)),
        check_vma=False,
    )
```

```python
import functools

import jax
import jax.numpy as jnp
from jax import lax
from jax.experimental import pallas as pl
from jax.experimental.pallas import tpu as pltpu
from jax.sharding import PartitionSpec as P

DH = 128
WIN = 4
PIECES = 10
AHEAD = 4
LOG2E = 1.4426950408889634
MESH = pl.DeviceIdType.MESH


def block_kernel(
    n,
    owner_ref,
    mask_ref,
    lengths_ref,
    q_ref,
    kv_ref,
    frames_ref,
    past_ref,
    gain_ref,
    shift_ref,
    weight_ref,
    out_ref,
    decoded_ref,
    slots,
    relay,
    up_in,
    down_in,
    up_out,
    down_out,
    taps,
    weights_here,
    partial,
    recv,
    send,
    edge_recv,
    edge_send,
    weight_sem,
):
    tokens = q_ref.shape[0]
    frames, _, cols, channels = frames_ref.shape
    past = past_ref.shape[0]
    padded = taps.shape[2]
    rows = n // 4
    width = q_ref.shape[1] // PIECES
    me = lax.axis_index("span")
    role = lax.rem(me, 4)
    z = me // 4

    def at(offset):
        return lax.rem(me + offset + n, n)

    def columns(piece):
        return pl.ds(pl.multiple_of(piece * width, width), width)

    def own(piece):
        return kv_ref.at[:, :, columns(piece)]

    def to_slot(source, slot, piece, lane, offset):
        return pltpu.make_async_remote_copy(
            src_ref=source,
            dst_ref=slots.at[slot, piece],
            send_sem=send.at[lane, piece],
            recv_sem=recv.at[slot, piece],
            device_id={"span": at(offset)},
            device_id_type=MESH,
        )

    def wave(source, target, kind, piece, offset):
        return pltpu.make_async_remote_copy(
            src_ref=source.at[piece],
            dst_ref=target.at[piece],
            send_sem=send.at[kind, piece],
            recv_sem=recv.at[kind, piece],
            device_id={"span": at(offset)},
            device_id_type=MESH,
        )

    def arrived(slot, piece):
        to_slot(slots.at[slot, piece], slot, piece, 0, 1).wait_recv()

    def edge(which):
        return pltpu.make_async_remote_copy(
            src_ref=taps.at[1],
            dst_ref=taps.at[2 * which],
            send_sem=edge_send.at[which],
            recv_sem=edge_recv.at[which],
            device_id={"span": at(1 - 2 * which)},
            device_id_type=MESH,
        )

    weight_copy = pltpu.make_async_copy(weight_ref, weights_here, weight_sem)
    weight_copy.start()

    barrier = pltpu.get_barrier_semaphore()
    for offset in (-4, -3, -2, -1, 1, 2, 3, 4):
        pl.semaphore_signal(barrier, inc=1, device_id={"span": at(offset)}, device_id_type=MESH)
    pl.semaphore_wait(barrier, 8)

    direct = {
        0: ((1, 1, 2), (0, 0, 1)),
        1: ((2, 0, 3), (1, 1, 2)),
        2: ((0, 0, 1),),
        3: ((2, 0, 3),),
    }

    def even(piece):
        return lax.rem(piece, 2) == 0

    def to_relay(piece, offset):
        return pltpu.make_async_remote_copy(
            src_ref=own(piece),
            dst_ref=relay.at[piece],
            send_sem=send.at[1, piece],
            recv_sem=recv.at[6, piece],
            device_id={"span": at(offset)},
            device_id_type=MESH,
        )

    def relayed(piece):
        return ((role == 0) & even(piece)) | ((role == 2) & jnp.logical_not(even(piece)))

    def pass_relayed(piece):
        @pl.when(relayed(piece))
        def _():
            to_relay(piece, 1).wait_recv()

        @pl.when((role == 0) & even(piece))
        def _():
            to_slot(relay.at[piece], 1, piece, 8, 4).start()

        @pl.when((role == 2) & jnp.logical_not(even(piece)))
        def _():
            to_slot(relay.at[piece], 1, piece, 8, -2).start()

    def send_own(piece):
        @pl.when((role == 2) & even(piece))
        def _():
            to_relay(piece, -2).start()

        @pl.when((role == 2) & jnp.logical_not(even(piece)))
        def _():
            to_relay(piece, 4).start()

        for which, copies in direct.items():

            @pl.when(role == which)
            def _():
                for slot, lane, offset in copies:
                    to_slot(own(piece), slot, piece, lane, offset).start()

    passed = {
        0: ((1, 2, 2, 1), (0, 1, 3, 1)),
        2: ((2, 0, 2, -2), (1, 2, 3, 1)),
        3: ((1, 0, 2, -1),),
    }
    kept = {0: (2,), 1: (0, 1, 2), 2: (0,), 3: (0, 2)}

    def window(piece):
        pass_relayed(piece)
        for which in range(4):

            @pl.when(role == which)
            def _():
                for slot, there, lane, offset in passed.get(which, ()):
                    arrived(slot, piece)
                    to_slot(slots.at[slot, piece], there, piece, lane, offset).start()
                for slot in kept[which]:
                    arrived(slot, piece)

    anchor = owner_ref[0]
    behind = lax.rem(me - anchor + n, n)
    group = jnp.where(role == 0, lax.rem((anchor + 3) // 4, rows), anchor // 4)

    def mine(piece, part):
        value = jnp.where(behind == 2, slots[1, piece, part], slots[2, piece, part])
        value = jnp.where(behind == 1, slots[0, piece, part], value)
        return jnp.where(behind == 0, kv_ref[part, :, columns(piece)], value)

    def crosses(piece):
        return lax.rem(piece, 5) == 1

    def crosses_back(piece):
        return lax.rem(piece, 5) == 3

    def waves(piece):
        upper = (role == 3) & jnp.logical_not(crosses_back(piece))
        return upper | ((role == 0) & jnp.logical_not(crosses(piece)))

    def within(piece):
        return (piece >= 0) & (piece < PIECES)

    position = lax.rem(me - anchor - 1 + 2 * n, n)
    length = lengths_ref[me]
    limits = [length]
    for offset in range(1, WIN):
        allowed = (position >= offset) & (mask_ref[position, offset - 1] == 1)
        limits.append(jnp.where(allowed, lengths_ref[at(-offset)], 0))
    limits.append(jnp.where(behind == 0, 0, lengths_ref[anchor]))

    def activate():
        spare = partial.at[0, 0, 0:padded, :]
        for frame in range(past + frames):
            if frame < past:
                value = past_ref[frame, 0].astype(jnp.float32)
            else:
                value = frames_ref[frame - past, 0].astype(jnp.float32)
                squares = jnp.mean(value * value, axis=-1, keepdims=True)
                value = value * lax.rsqrt(squares + 1e-06) * gain_ref[...].reshape(1, channels)
                value = value / (1.0 + jnp.exp(-value))
            spare[...] = jnp.zeros(spare.shape, jnp.float32)
            spare[0:cols, :] = value
            taps[1, frame] = spare[...].astype(jnp.bfloat16)
        partial[0, :, 0:8, :] = jnp.zeros((frames, 8, channels), jnp.float32)

        @pl.when(me < n - 1)
        def _():
            edge(0).start()

        @pl.when(me > 0)
        def _():
            edge(1).start()

        @pl.when(me == 0)
        def _():
            taps[0] = jnp.zeros(taps.shape[1:], taps.dtype)

        @pl.when(me == n - 1)
        def _():
            taps[2] = jnp.zeros(taps.shape[1:], taps.dtype)

    def edges_arrived():
        @pl.when(me > 0)
        def _():
            edge(0).wait_recv()

        @pl.when(me < n - 1)
        def _():
            edge(1).wait_recv()

        weight_copy.wait()

    def convolve(col_tap):
        total = None
        for frame_tap in range(3):
            for row_tap in range(3):
                window_rows = taps[row_tap, frame_tap : frame_tap + frames]
                term = jnp.dot(
                    window_rows.reshape(frames * padded, channels),
                    weights_here[frame_tap, row_tap, col_tap],
                    preferred_element_type=jnp.float32,
                )
                total = term if total is None else total + term
        partial[col_tap, :, 8 : 8 + padded, :] = total.reshape(frames, padded, channels)

    def decode():
        for frame in range(frames):
            total = frames_ref[frame, 0].astype(jnp.float32) + shift_ref[...].reshape(1, channels)
            for col_tap in range(3):
                total = total + partial[col_tap, frame, 7 + col_tap : 7 + col_tap + cols, :]
            decoded_ref[frame, 0] = total.astype(decoded_ref.dtype)

    def attend(piece):
        token = lax.broadcasted_iota(jnp.int32, (1, tokens), 1)
        hidden = [jnp.where(token < limit, 0.0, -1e30) for limit in limits]
        row = lax.broadcasted_iota(jnp.int32, (tokens, 1), 0)
        for sub in range(width // DH):
            cols = pl.ds(pl.multiple_of(piece * width + sub * DH, DH), DH)
            inner = slice(sub * DH, (sub + 1) * DH)
            query = q_ref[:, cols]
            scores = []
            for block in range(5):
                key = kv_ref[0, :, cols] if block == 0 else slots[block - 1, piece, 0, :, inner]
                score = lax.dot_general(
                    query, key, (((1,), (1,)), ((), ())), preferred_element_type=jnp.float32
                )
                scores.append(score * (DH**-0.5 * LOG2E) + hidden[block])
            top = functools.reduce(jnp.maximum, scores)
            top = jnp.max(top, axis=-1, keepdims=True)
            weights = [jnp.exp2(score - top) for score in scores]
            total = jnp.sum(functools.reduce(jnp.add, weights), axis=-1, keepdims=True)
            blended = None
            for block in range(5):
                value = kv_ref[1, :, cols] if block == 0 else slots[block - 1, piece, 1, :, inner]
                term = jnp.dot(
                    weights[block].astype(jnp.bfloat16), value, preferred_element_type=jnp.float32
                )
                blended = term if blended is None else blended + term
            out_ref[:, cols] = jnp.where(row < length, blended / total, 0.0).astype(out_ref.dtype)

    def start(piece, _):
        send_own(piece)
        return 0

    lax.fori_loop(0, AHEAD, start, 0)
    activate()

    def step(t, _):
        @pl.when(t + AHEAD < PIECES)
        def _():
            send_own(t + AHEAD)

        @pl.when(t < PIECES)
        def _():
            window(t)

        @pl.when(t == 2)
        def _():
            edges_arrived()

        @pl.when((t >= 2) & (t < 5))
        def _():
            convolve(t - 2)

        @pl.when(t == 5)
        def _():
            decode()

        rising = t - z
        falling = t - (rows - 1 - z)
        final = t - (rows - 1)
        ready = t - rows

        @pl.when(within(rising) & waves(rising))
        def _():
            @pl.when(z > 0)
            def _():
                wave(up_out, up_in, 4, rising, 4).wait_recv()

            @pl.when(z < rows - 1)
            def _():
                for part in range(2):
                    up_out[rising, part] = jnp.where(
                        group == z, mine(rising, part), up_in[rising, part]
                    )
                wave(up_out, up_in, 4, rising, 4).start()

        @pl.when(within(falling) & waves(falling))
        def _():
            @pl.when(z < rows - 1)
            def _():
                wave(down_out, down_in, 5, falling, -4).wait_recv()

            @pl.when(z > 0)
            def _():
                for part in range(2):
                    down_out[falling, part] = jnp.where(
                        group == z, mine(falling, part), down_in[falling, part]
                    )
                wave(down_out, down_in, 5, falling, -4).start()

        @pl.when(within(final) & waves(final))
        def _():
            for part in range(2):
                value = jnp.where(group < z, up_in[final, part], down_in[final, part])
                slots[3, final, part] = jnp.where(group == z, mine(final, part), value)

            @pl.when((role == 3) & crosses(final))
            def _():
                to_slot(slots.at[3, final], 3, final, 7, -3).start()

            @pl.when((role == 0) & crosses_back(final))
            def _():
                to_slot(slots.at[3, final], 3, final, 7, 3).start()

            @pl.when(role == 3)
            def _():
                to_slot(slots.at[3, final], 3, final, 6, -1).start()

            @pl.when(role == 0)
            def _():
                to_slot(slots.at[3, final], 3, final, 6, 1).start()

        @pl.when(within(ready))
        def _():
            @pl.when((role == 0) & crosses(ready))
            def _():
                arrived(3, ready)
                to_slot(slots.at[3, ready], 3, ready, 6, 1).start()

            @pl.when((role == 3) & crosses_back(ready))
            def _():
                arrived(3, ready)
                to_slot(slots.at[3, ready], 3, ready, 6, -1).start()

            @pl.when((role == 1) | (role == 2))
            def _():
                arrived(3, ready)

            attend(ready)

        return 0

    lax.fori_loop(0, PIECES + rows, step, 0)

    def finish(piece, _):
        for which in range(4):

            @pl.when(role == which)
            def _():
                for slot, lane, offset in direct[which]:
                    to_slot(own(piece), slot, piece, lane, offset).wait_send()
                for slot, there, lane, offset in passed.get(which, ()):
                    to_slot(slots.at[slot, piece], there, piece, lane, offset).wait_send()

        @pl.when(waves(piece) & (z < rows - 1))
        def _():
            wave(up_out, up_in, 4, piece, 4).wait_send()

        @pl.when(waves(piece) & (z > 0))
        def _():
            wave(down_out, down_in, 5, piece, -4).wait_send()

        @pl.when((role == 0) | (role == 3))
        def _():
            to_slot(slots.at[3, piece], 3, piece, 6, 1).wait_send()

        @pl.when(((role == 3) & crosses(piece)) | ((role == 0) & crosses_back(piece)))
        def _():
            to_slot(slots.at[3, piece], 3, piece, 7, -3).wait_send()

        @pl.when(role == 2)
        def _():
            to_relay(piece, 4).wait_send()

        @pl.when(relayed(piece))
        def _():
            to_slot(relay.at[piece], 1, piece, 8, 4).wait_send()

        return 0

    lax.fori_loop(0, PIECES, finish, 0)

    @pl.when(me < n - 1)
    def _():
        edge(0).wait_send()

    @pl.when(me > 0)
    def _():
        edge(1).wait_send()


def shards(
    queries,
    keys_values,
    owner,
    span_mask,
    lengths,
    frames,
    past_frames,
    norm_gain,
    conv_weight,
    conv_bias,
):
    n = lax.axis_size("span")
    rows, cols = queries.shape
    piece = (PIECES, 2, rows, cols // PIECES)
    frame_count, _, frame_cols, channels = frames.shape
    padded = -(-(frame_cols + 1) // 16) * 16
    attention_flops = 4 * rows * 5 * rows * cols
    conv_flops = 2 * frame_count * frame_cols * conv_weight.size
    scalars = pl.BlockSpec(memory_space=pltpu.SMEM)
    whole = pl.BlockSpec(memory_space=pltpu.VMEM)
    return pl.pallas_call(
        functools.partial(block_kernel, n),
        out_shape=(
            jax.ShapeDtypeStruct((rows, cols), jnp.bfloat16),
            jax.ShapeDtypeStruct(frames.shape, jnp.bfloat16),
        ),
        in_specs=[scalars] * 3 + [whole] * 6 + [pl.BlockSpec(memory_space=pl.ANY)],
        out_specs=(whole, whole),
        scratch_shapes=[
            pltpu.VMEM((4,) + piece, jnp.bfloat16),
            pltpu.VMEM(piece, jnp.bfloat16),
            pltpu.VMEM(piece, jnp.bfloat16),
            pltpu.VMEM(piece, jnp.bfloat16),
            pltpu.VMEM(piece, jnp.bfloat16),
            pltpu.VMEM(piece, jnp.bfloat16),
            pltpu.VMEM((3, frame_count + past_frames.shape[0], padded, channels), jnp.bfloat16),
            pltpu.VMEM(conv_weight.shape, jnp.bfloat16),
            pltpu.VMEM((3, frame_count, padded + 16, channels), jnp.float32),
            pltpu.SemaphoreType.DMA((7, PIECES)),
            pltpu.SemaphoreType.DMA((9, PIECES)),
            pltpu.SemaphoreType.DMA((2,)),
            pltpu.SemaphoreType.DMA((2,)),
            pltpu.SemaphoreType.DMA,
        ],
        cost_estimate=pl.CostEstimate(
            flops=attention_flops + conv_flops,
            bytes_accessed=8 * rows * cols + 2 * conv_weight.size,
            transcendentals=5 * rows * rows * cols // DH,
        ),
        compiler_params=pltpu.CompilerParams(
            collective_id=0, has_side_effects=True, vmem_limit_bytes=60 * 1024 * 1024
        ),
        name="spans_and_decoder",
    )(
        owner,
        span_mask,
        lengths,
        queries,
        keys_values,
        frames,
        past_frames,
        norm_gain,
        conv_bias,
        conv_weight,
    )


def solution(mesh):
    placed = (
        P(("group", "span"), None),
        P(None, ("group", "span"), None),
        P("group"),
        P("group", None),
        P("group"),
        P("group", "span", None, None),
        P("group", "span", None, None),
        P(),
        P(),
        P(),
    )
    return jax.shard_map(
        shards,
        mesh=mesh,
        in_specs=placed,
        out_specs=(P(("group", "span"), None), P("group", "span", None, None)),
        check_vma=False,
    )
```

```python
import functools

import jax
import jax.numpy as jnp
from jax import lax
from jax.experimental import pallas as pl
from jax.experimental.pallas import tpu as pltpu
from jax.sharding import PartitionSpec as P

DH = 128
WIN = 4
PIECES = 20
AHEAD = 4
HOP = 2
LOG2E = 1.4426950408889634
MESH = pl.DeviceIdType.MESH


def block_kernel(
    n,
    owner_ref,
    mask_ref,
    lengths_ref,
    q_ref,
    kv_ref,
    frames_ref,
    past_ref,
    gain_ref,
    shift_ref,
    weight_ref,
    out_ref,
    decoded_ref,
    slots,
    relay,
    up_in,
    down_in,
    up_out,
    down_out,
    taps,
    weights_here,
    partial,
    recv,
    send,
    edge_recv,
    edge_send,
    weight_sem,
):
    tokens = q_ref.shape[0]
    frames, _, cols, channels = frames_ref.shape
    past = past_ref.shape[0]
    padded = taps.shape[2]
    rows = n // 4
    width = q_ref.shape[1] // PIECES
    me = lax.axis_index("span")
    role = lax.rem(me, 4)
    z = me // 4

    def at(offset):
        return lax.rem(me + offset + n, n)

    def columns(piece):
        return pl.ds(pl.multiple_of(piece * width, width), width)

    def own(piece):
        return kv_ref.at[:, :, columns(piece)]

    def to_slot(source, slot, piece, lane, offset):
        return pltpu.make_async_remote_copy(
            src_ref=source,
            dst_ref=slots.at[slot, piece],
            send_sem=send.at[lane, piece],
            recv_sem=recv.at[slot, piece],
            device_id={"span": at(offset)},
            device_id_type=MESH,
        )

    def wave(source, target, kind, piece, offset):
        return pltpu.make_async_remote_copy(
            src_ref=source.at[piece],
            dst_ref=target.at[piece],
            send_sem=send.at[kind, piece],
            recv_sem=recv.at[kind, piece],
            device_id={"span": at(offset)},
            device_id_type=MESH,
        )

    def arrived(slot, piece):
        to_slot(slots.at[slot, piece], slot, piece, 0, 1).wait_recv()

    def edge(which):
        return pltpu.make_async_remote_copy(
            src_ref=taps.at[1],
            dst_ref=taps.at[2 * which],
            send_sem=edge_send.at[which],
            recv_sem=edge_recv.at[which],
            device_id={"span": at(1 - 2 * which)},
            device_id_type=MESH,
        )

    weight_copy = pltpu.make_async_copy(weight_ref, weights_here, weight_sem)
    weight_copy.start()

    barrier = pltpu.get_barrier_semaphore()
    for offset in (-4, -3, -2, -1, 1, 2, 3, 4):
        pl.semaphore_signal(barrier, inc=1, device_id={"span": at(offset)}, device_id_type=MESH)
    pl.semaphore_wait(barrier, 8)

    direct = {
        0: ((1, 1, 2), (0, 0, 1)),
        1: ((2, 0, 3), (1, 1, 2)),
        2: ((0, 0, 1),),
        3: ((2, 0, 3),),
    }

    def even(piece):
        return lax.rem(piece, 2) == 0

    def to_relay(piece, offset):
        return pltpu.make_async_remote_copy(
            src_ref=own(piece),
            dst_ref=relay.at[piece],
            send_sem=send.at[1, piece],
            recv_sem=recv.at[6, piece],
            device_id={"span": at(offset)},
            device_id_type=MESH,
        )

    def relayed(piece):
        return ((role == 0) & even(piece)) | ((role == 2) & jnp.logical_not(even(piece)))

    def pass_relayed(piece):
        @pl.when(relayed(piece))
        def _():
            to_relay(piece, 1).wait_recv()

        @pl.when((role == 0) & even(piece))
        def _():
            to_slot(relay.at[piece], 1, piece, 8, 4).start()

        @pl.when((role == 2) & jnp.logical_not(even(piece)))
        def _():
            to_slot(relay.at[piece], 1, piece, 8, -2).start()

    def send_own(piece):
        @pl.when((role == 2) & even(piece))
        def _():
            to_relay(piece, -2).start()

        @pl.when((role == 2) & jnp.logical_not(even(piece)))
        def _():
            to_relay(piece, 4).start()

        for which, copies in direct.items():

            @pl.when(role == which)
            def _():
                for slot, lane, offset in copies:
                    to_slot(own(piece), slot, piece, lane, offset).start()

    passed = {2: ((2, 0, 2, -2), (1, 2, 3, 1)), 3: ((1, 0, 2, -1),)}
    passed_again = {0: ((1, 2, 2, 1), (0, 1, 3, 1))}
    kept = {0: (2,), 2: (0,), 3: (0, 2)}

    def pass_on(piece, table):
        for which, copies in table.items():

            @pl.when(role == which)
            def _():
                for slot, there, lane, offset in copies:
                    arrived(slot, piece)
                    to_slot(slots.at[slot, piece], there, piece, lane, offset).start()

    def keep(piece):
        for which, slots_here in kept.items():

            @pl.when(role == which)
            def _():
                for slot in slots_here:
                    arrived(slot, piece)

    anchor = owner_ref[0]
    behind = lax.rem(me - anchor + n, n)
    group = jnp.where(role == 0, lax.rem((anchor + 3) // 4, rows), anchor // 4)

    def mine(piece, part):
        value = jnp.where(behind == 2, slots[1, piece, part], slots[2, piece, part])
        value = jnp.where(behind == 1, slots[0, piece, part], value)
        return jnp.where(behind == 0, kv_ref[part, :, columns(piece)], value)

    def crosses(piece):
        return lax.rem(piece, 5) == 1

    def crosses_back(piece):
        return lax.rem(piece, 5) == 3

    def waves(piece):
        upper = (role == 3) & jnp.logical_not(crosses_back(piece))
        return upper | ((role == 0) & jnp.logical_not(crosses(piece)))

    def within(piece):
        return (piece >= 0) & (piece < PIECES)

    position = lax.rem(me - anchor - 1 + 2 * n, n)
    length = lengths_ref[me]
    limits = [length]
    for offset in range(1, WIN):
        allowed = (position >= offset) & (mask_ref[position, offset - 1] == 1)
        limits.append(jnp.where(allowed, lengths_ref[at(-offset)], 0))
    limits.append(jnp.where(behind == 0, 0, lengths_ref[anchor]))

    def activate():
        spare = partial.at[0, 0, 0:padded, :]
        for frame in range(past + frames):
            if frame < past:
                value = past_ref[frame, 0].astype(jnp.float32)
            else:
                value = frames_ref[frame - past, 0].astype(jnp.float32)
                squares = jnp.mean(value * value, axis=-1, keepdims=True)
                value = value * lax.rsqrt(squares + 1e-06) * gain_ref[...].reshape(1, channels)
                value = value / (1.0 + jnp.exp(-value))
            spare[...] = jnp.zeros(spare.shape, jnp.float32)
            spare[0:cols, :] = value
            taps[1, frame] = spare[...].astype(jnp.bfloat16)
        partial[0, :, 0:8, :] = jnp.zeros((frames, 8, channels), jnp.float32)

        @pl.when(me < n - 1)
        def _():
            edge(0).start()

        @pl.when(me > 0)
        def _():
            edge(1).start()

        @pl.when(me == 0)
        def _():
            taps[0] = jnp.zeros(taps.shape[1:], taps.dtype)

        @pl.when(me == n - 1)
        def _():
            taps[2] = jnp.zeros(taps.shape[1:], taps.dtype)

    def edges_arrived():
        @pl.when(me > 0)
        def _():
            edge(0).wait_recv()

        @pl.when(me < n - 1)
        def _():
            edge(1).wait_recv()

        weight_copy.wait()

    def convolve(col_tap):
        total = None
        for frame_tap in range(3):
            for row_tap in range(3):
                window_rows = taps[row_tap, frame_tap : frame_tap + frames]
                term = jnp.dot(
                    window_rows.reshape(frames * padded, channels),
                    weights_here[frame_tap, row_tap, col_tap],
                    preferred_element_type=jnp.float32,
                )
                total = term if total is None else total + term
        partial[col_tap, :, 8 : 8 + padded, :] = total.reshape(frames, padded, channels)

    def decode():
        for frame in range(frames):
            total = frames_ref[frame, 0].astype(jnp.float32) + shift_ref[...].reshape(1, channels)
            for col_tap in range(3):
                total = total + partial[col_tap, frame, 7 + col_tap : 7 + col_tap + cols, :]
            decoded_ref[frame, 0] = total.astype(decoded_ref.dtype)

    def attend(piece):
        token = lax.broadcasted_iota(jnp.int32, (1, tokens), 1)
        hidden = [jnp.where(token < limit, 0.0, -1e30) for limit in limits]
        row = lax.broadcasted_iota(jnp.int32, (tokens, 1), 0)
        for sub in range(width // DH):
            cols = pl.ds(pl.multiple_of(piece * width + sub * DH, DH), DH)
            inner = slice(sub * DH, (sub + 1) * DH)
            query = q_ref[:, cols]
            scores = []
            for block in range(5):
                key = kv_ref[0, :, cols] if block == 0 else slots[block - 1, piece, 0, :, inner]
                score = lax.dot_general(
                    query, key, (((1,), (1,)), ((), ())), preferred_element_type=jnp.float32
                )
                scores.append(score * (DH**-0.5 * LOG2E) + hidden[block])
            top = functools.reduce(jnp.maximum, scores)
            top = jnp.max(top, axis=-1, keepdims=True)
            weights = [jnp.exp2(score - top) for score in scores]
            total = jnp.sum(functools.reduce(jnp.add, weights), axis=-1, keepdims=True)
            blended = None
            for block in range(5):
                value = kv_ref[1, :, cols] if block == 0 else slots[block - 1, piece, 1, :, inner]
                term = jnp.dot(
                    weights[block].astype(jnp.bfloat16), value, preferred_element_type=jnp.float32
                )
                blended = term if blended is None else blended + term
            out_ref[:, cols] = jnp.where(row < length, blended / total, 0.0).astype(out_ref.dtype)

    def start(piece, _):
        send_own(piece)
        return 0

    lax.fori_loop(0, AHEAD, start, 0)
    activate()

    def step(t, _):
        @pl.when(t + AHEAD < PIECES)
        def _():
            send_own(t + AHEAD)

        @pl.when(t < PIECES)
        def _():
            pass_on(t, passed)
            pass_relayed(t)

        known = t - 1

        @pl.when(within(known))
        def _():
            pass_on(known, passed_again)
            keep(known)

        @pl.when(t == 2)
        def _():
            edges_arrived()

        @pl.when((t >= 2) & (t < 5))
        def _():
            convolve(t - 2)

        @pl.when(t == 5)
        def _():
            decode()

        rising = known - HOP * z
        falling = known - HOP * (rows - 1 - z)
        final = known - HOP * (rows - 1)
        crossed = final - 1
        ready = final - 2

        @pl.when(within(rising) & waves(rising))
        def _():
            @pl.when(z > 0)
            def _():
                wave(up_out, up_in, 4, rising, 4).wait_recv()

            @pl.when(z < rows - 1)
            def _():
                for part in range(2):
                    up_out[rising, part] = jnp.where(
                        group == z, mine(rising, part), up_in[rising, part]
                    )
                wave(up_out, up_in, 4, rising, 4).start()

        @pl.when(within(falling) & waves(falling))
        def _():
            @pl.when(z < rows - 1)
            def _():
                wave(down_out, down_in, 5, falling, -4).wait_recv()

            @pl.when(z > 0)
            def _():
                for part in range(2):
                    down_out[falling, part] = jnp.where(
                        group == z, mine(falling, part), down_in[falling, part]
                    )
                wave(down_out, down_in, 5, falling, -4).start()

        @pl.when(within(final) & waves(final))
        def _():
            for part in range(2):
                value = jnp.where(group < z, up_in[final, part], down_in[final, part])
                slots[3, final, part] = jnp.where(group == z, mine(final, part), value)

            @pl.when((role == 3) & crosses(final))
            def _():
                to_slot(slots.at[3, final], 3, final, 7, -3).start()

            @pl.when((role == 0) & crosses_back(final))
            def _():
                to_slot(slots.at[3, final], 3, final, 7, 3).start()

            @pl.when(role == 3)
            def _():
                to_slot(slots.at[3, final], 3, final, 6, -1).start()

            @pl.when(role == 0)
            def _():
                to_slot(slots.at[3, final], 3, final, 6, 1).start()

        @pl.when(within(crossed) & (role == 0) & crosses(crossed))
        def _():
            arrived(3, crossed)
            to_slot(slots.at[3, crossed], 3, crossed, 6, 1).start()

        @pl.when(within(crossed) & (role == 3) & crosses_back(crossed))
        def _():
            arrived(3, crossed)
            to_slot(slots.at[3, crossed], 3, crossed, 6, -1).start()

        @pl.when(within(ready))
        def _():
            @pl.when(role == 1)
            def _():
                for slot in range(3):
                    arrived(slot, ready)

            @pl.when((role == 1) | (role == 2))
            def _():
                arrived(3, ready)

            attend(ready)

        return 0

    lax.fori_loop(0, PIECES + 3 + HOP * (rows - 1), step, 0)

    def finish(piece, _):
        for which in range(4):

            @pl.when(role == which)
            def _():
                for slot, lane, offset in direct[which]:
                    to_slot(own(piece), slot, piece, lane, offset).wait_send()
                for slot, there, lane, offset in passed.get(which, ()) + passed_again.get(which, ()):
                    to_slot(slots.at[slot, piece], there, piece, lane, offset).wait_send()

        @pl.when(waves(piece) & (z < rows - 1))
        def _():
            wave(up_out, up_in, 4, piece, 4).wait_send()

        @pl.when(waves(piece) & (z > 0))
        def _():
            wave(down_out, down_in, 5, piece, -4).wait_send()

        @pl.when((role == 0) | (role == 3))
        def _():
            to_slot(slots.at[3, piece], 3, piece, 6, 1).wait_send()

        @pl.when(((role == 3) & crosses(piece)) | ((role == 0) & crosses_back(piece)))
        def _():
            to_slot(slots.at[3, piece], 3, piece, 7, -3).wait_send()

        @pl.when(role == 2)
        def _():
            to_relay(piece, 4).wait_send()

        @pl.when(relayed(piece))
        def _():
            to_slot(relay.at[piece], 1, piece, 8, 4).wait_send()

        return 0

    lax.fori_loop(0, PIECES, finish, 0)

    @pl.when(me < n - 1)
    def _():
        edge(0).wait_send()

    @pl.when(me > 0)
    def _():
        edge(1).wait_send()


def shards(
    queries,
    keys_values,
    owner,
    span_mask,
    lengths,
    frames,
    past_frames,
    norm_gain,
    conv_weight,
    conv_bias,
):
    n = lax.axis_size("span")
    rows, cols = queries.shape
    piece = (PIECES, 2, rows, cols // PIECES)
    frame_count, _, frame_cols, channels = frames.shape
    padded = -(-(frame_cols + 1) // 16) * 16
    attention_flops = 4 * rows * 5 * rows * cols
    conv_flops = 2 * frame_count * frame_cols * conv_weight.size
    scalars = pl.BlockSpec(memory_space=pltpu.SMEM)
    whole = pl.BlockSpec(memory_space=pltpu.VMEM)
    return pl.pallas_call(
        functools.partial(block_kernel, n),
        out_shape=(
            jax.ShapeDtypeStruct((rows, cols), jnp.bfloat16),
            jax.ShapeDtypeStruct(frames.shape, jnp.bfloat16),
        ),
        in_specs=[scalars] * 3 + [whole] * 6 + [pl.BlockSpec(memory_space=pl.ANY)],
        out_specs=(whole, whole),
        scratch_shapes=[
            pltpu.VMEM((4,) + piece, jnp.bfloat16),
            pltpu.VMEM(piece, jnp.bfloat16),
            pltpu.VMEM(piece, jnp.bfloat16),
            pltpu.VMEM(piece, jnp.bfloat16),
            pltpu.VMEM(piece, jnp.bfloat16),
            pltpu.VMEM(piece, jnp.bfloat16),
            pltpu.VMEM((3, frame_count + past_frames.shape[0], padded, channels), jnp.bfloat16),
            pltpu.VMEM(conv_weight.shape, jnp.bfloat16),
            pltpu.VMEM((3, frame_count, padded + 16, channels), jnp.float32),
            pltpu.SemaphoreType.DMA((7, PIECES)),
            pltpu.SemaphoreType.DMA((9, PIECES)),
            pltpu.SemaphoreType.DMA((2,)),
            pltpu.SemaphoreType.DMA((2,)),
            pltpu.SemaphoreType.DMA,
        ],
        cost_estimate=pl.CostEstimate(
            flops=attention_flops + conv_flops,
            bytes_accessed=8 * rows * cols + 2 * conv_weight.size,
            transcendentals=5 * rows * rows * cols // DH,
        ),
        compiler_params=pltpu.CompilerParams(
            collective_id=0, has_side_effects=True, vmem_limit_bytes=60 * 1024 * 1024
        ),
        name="spans_and_decoder",
    )(
        owner,
        span_mask,
        lengths,
        queries,
        keys_values,
        frames,
        past_frames,
        norm_gain,
        conv_bias,
        conv_weight,
    )


def solution(mesh):
    placed = (
        P(("group", "span"), None),
        P(None, ("group", "span"), None),
        P("group"),
        P("group", None),
        P("group"),
        P("group", "span", None, None),
        P("group", "span", None, None),
        P(),
        P(),
        P(),
    )
    return jax.shard_map(
        shards,
        mesh=mesh,
        in_specs=placed,
        out_specs=(P(("group", "span"), None), P("group", "span", None, None)),
        check_vma=False,
    )
```

```python
import functools

import jax
import jax.numpy as jnp
from jax import lax
from jax.experimental import pallas as pl
from jax.experimental.pallas import tpu as pltpu
from jax.sharding import PartitionSpec as P

DH = 128
WIN = 4
PIECES = 20
AHEAD = 4
HOP = 2
LAG = 2
LOG2E = 1.4426950408889634
MESH = pl.DeviceIdType.MESH


def block_kernel(
    n,
    owner_ref,
    mask_ref,
    lengths_ref,
    q_ref,
    kv_ref,
    frames_ref,
    past_ref,
    gain_ref,
    shift_ref,
    weight_ref,
    out_ref,
    decoded_ref,
    limit_ref,
    slots,
    relay,
    up_in,
    down_in,
    up_out,
    down_out,
    taps,
    weights_here,
    partial,
    recv,
    send,
    edge_recv,
    edge_send,
    weight_sem,
):
    tokens = q_ref.shape[0]
    frames, _, cols, channels = frames_ref.shape
    past = past_ref.shape[2]
    padded = taps.shape[2]
    rows = n // 4
    width = q_ref.shape[1] // PIECES
    me = lax.axis_index("span")
    role = lax.rem(me, 4)
    z = me // 4

    def at(offset):
        return lax.rem(me + offset + n, n)

    def columns(piece):
        return pl.ds(pl.multiple_of(piece * width, width), width)

    def own(piece):
        return kv_ref.at[:, :, columns(piece)]

    def to_slot(source, slot, piece, lane, offset):
        return pltpu.make_async_remote_copy(
            src_ref=source,
            dst_ref=slots.at[slot, piece],
            send_sem=send.at[lane, piece],
            recv_sem=recv.at[slot, piece],
            device_id={"span": at(offset)},
            device_id_type=MESH,
        )

    def wave(source, target, kind, piece, offset):
        return pltpu.make_async_remote_copy(
            src_ref=source.at[piece],
            dst_ref=target.at[piece],
            send_sem=send.at[kind, piece],
            recv_sem=recv.at[kind, piece],
            device_id={"span": at(offset)},
            device_id_type=MESH,
        )

    def arrived(slot, piece):
        to_slot(slots.at[slot, piece], slot, piece, 0, 1).wait_recv()

    def edge(which):
        return pltpu.make_async_remote_copy(
            src_ref=taps.at[1],
            dst_ref=taps.at[2 * which],
            send_sem=edge_send.at[which],
            recv_sem=edge_recv.at[which],
            device_id={"span": at(1 - 2 * which)},
            device_id_type=MESH,
        )

    weight_copy = pltpu.make_async_copy(weight_ref, weights_here, weight_sem)
    weight_copy.start()

    barrier = pltpu.get_barrier_semaphore()
    for offset in (-4, -3, -2, -1, 1, 2, 3, 4):
        pl.semaphore_signal(barrier, inc=1, device_id={"span": at(offset)}, device_id_type=MESH)
    pl.semaphore_wait(barrier, 8)

    direct = {
        0: ((1, 1, 2), (0, 0, 1)),
        1: ((2, 0, 3), (1, 1, 2)),
        2: ((0, 0, 1),),
        3: ((2, 0, 3),),
    }

    def even(piece):
        return lax.rem(piece, 2) == 0

    def to_relay(piece, offset):
        return pltpu.make_async_remote_copy(
            src_ref=own(piece),
            dst_ref=relay.at[piece],
            send_sem=send.at[1, piece],
            recv_sem=recv.at[6, piece],
            device_id={"span": at(offset)},
            device_id_type=MESH,
        )

    def relayed(piece):
        return ((role == 0) & even(piece)) | ((role == 2) & jnp.logical_not(even(piece)))

    def pass_relayed(piece):
        @pl.when(relayed(piece))
        def _():
            to_relay(piece, 1).wait_recv()

        @pl.when((role == 0) & even(piece))
        def _():
            to_slot(relay.at[piece], 1, piece, 8, 4).start()

        @pl.when((role == 2) & jnp.logical_not(even(piece)))
        def _():
            to_slot(relay.at[piece], 1, piece, 8, -2).start()

    def send_own(piece):
        @pl.when((role == 2) & even(piece))
        def _():
            to_relay(piece, -2).start()

        @pl.when((role == 2) & jnp.logical_not(even(piece)))
        def _():
            to_relay(piece, 4).start()

        for which, copies in direct.items():

            @pl.when(role == which)
            def _():
                for slot, lane, offset in copies:
                    to_slot(own(piece), slot, piece, lane, offset).start()

    passed = {2: ((2, 0, 2, -2), (1, 2, 3, 1)), 3: ((1, 0, 2, -1),)}
    passed_again = {0: ((1, 2, 2, 1), (0, 1, 3, 1))}
    kept = {0: (2,), 2: (0,), 3: (0, 2)}

    def pass_on(piece, table):
        for which, copies in table.items():

            @pl.when(role == which)
            def _():
                for slot, there, lane, offset in copies:
                    arrived(slot, piece)
                    to_slot(slots.at[slot, piece], there, piece, lane, offset).start()

    def keep(piece):
        for which, slots_here in kept.items():

            @pl.when(role == which)
            def _():
                for slot in slots_here:
                    arrived(slot, piece)

    anchor = owner_ref[0]
    behind = lax.rem(me - anchor + n, n)
    group = jnp.where(role == 0, lax.rem((anchor + 3) // 4, rows), anchor // 4)

    def mine(piece, part):
        value = jnp.where(behind == 2, slots[1, piece, part], slots[2, piece, part])
        value = jnp.where(behind == 1, slots[0, piece, part], value)
        return jnp.where(behind == 0, kv_ref[part, :, columns(piece)], value)

    def crosses(piece):
        return lax.rem(piece, 5) == 1

    def crosses_back(piece):
        return lax.rem(piece, 5) == 3

    def waves(piece):
        upper = (role == 3) & jnp.logical_not(crosses_back(piece))
        return upper | ((role == 0) & jnp.logical_not(crosses(piece)))

    def within(piece):
        return (piece >= 0) & (piece < PIECES)

    position = lax.rem(me - anchor - 1 + 2 * n, n)
    length = lengths_ref[me]
    limit_ref[...] = jnp.full(limit_ref.shape, length, jnp.int32)
    limits = [length]
    for offset in range(1, WIN):
        allowed = (position >= offset) & (mask_ref[offset - 1, position] == 1)
        limits.append(jnp.where(allowed, lengths_ref[at(-offset)], 0))
    limits.append(jnp.where(behind == 0, 0, lengths_ref[anchor]))

    def activate():
        spare = partial.at[0, 0, 0:padded, :]
        for frame in range(past + frames):
            if frame < past:
                value = past_ref[0].astype(jnp.float32)[:, frame, :]
            else:
                value = frames_ref[frame - past, 0].astype(jnp.float32)
                squares = jnp.mean(value * value, axis=-1, keepdims=True)
                value = value * lax.rsqrt(squares + 1e-06) * gain_ref[...].reshape(1, channels)
                value = value / (1.0 + jnp.exp(-value))
            spare[...] = jnp.zeros(spare.shape, jnp.float32)
            spare[0:cols, :] = value
            taps[1, frame] = spare[...].astype(jnp.bfloat16)
        partial[0, :, 0:8, :] = jnp.zeros((frames, 8, channels), jnp.float32)

        @pl.when(me < n - 1)
        def _():
            edge(0).start()

        @pl.when(me > 0)
        def _():
            edge(1).start()

        @pl.when(me == 0)
        def _():
            taps[0] = jnp.zeros(taps.shape[1:], taps.dtype)

        @pl.when(me == n - 1)
        def _():
            taps[2] = jnp.zeros(taps.shape[1:], taps.dtype)

    def edges_arrived():
        @pl.when(me > 0)
        def _():
            edge(0).wait_recv()

        @pl.when(me < n - 1)
        def _():
            edge(1).wait_recv()

        weight_copy.wait()

    def convolve(col_tap):
        total = None
        for frame_tap in range(3):
            for row_tap in range(3):
                window_rows = taps[row_tap, frame_tap : frame_tap + frames]
                term = jnp.dot(
                    window_rows.reshape(frames * padded, channels),
                    weights_here[frame_tap, row_tap, col_tap],
                    preferred_element_type=jnp.float32,
                )
                total = term if total is None else total + term
        partial[col_tap, :, 8 : 8 + padded, :] = total.reshape(frames, padded, channels)

    def decode():
        for frame in range(frames):
            total = frames_ref[frame, 0].astype(jnp.float32) + shift_ref[...].reshape(1, channels)
            for col_tap in range(3):
                total = total + partial[col_tap, frame, 7 + col_tap : 7 + col_tap + cols, :]
            decoded_ref[frame, 0] = total.astype(decoded_ref.dtype)

    def attend(piece):
        token = lax.broadcasted_iota(jnp.int32, (1, tokens), 1)
        hidden = [jnp.where(token < limit, 0.0, -1e30) for limit in limits]
        for sub in range(width // DH):
            cols = pl.ds(pl.multiple_of(piece * width + sub * DH, DH), DH)
            inner = slice(sub * DH, (sub + 1) * DH)
            query = q_ref[:, cols]
            scores = []
            for block in range(5):
                key = kv_ref[0, :, cols] if block == 0 else slots[block - 1, piece, 0, :, inner]
                score = lax.dot_general(
                    query, key, (((1,), (1,)), ((), ())), preferred_element_type=jnp.float32
                )
                scores.append(score * (DH**-0.5 * LOG2E) + hidden[block])
            top = functools.reduce(jnp.maximum, scores)
            top = jnp.max(top, axis=-1, keepdims=True)
            weights = [jnp.exp2(score - top) for score in scores]
            total = jnp.sum(functools.reduce(jnp.add, weights), axis=-1, keepdims=True)
            blended = None
            for block in range(5):
                value = kv_ref[1, :, cols] if block == 0 else slots[block - 1, piece, 1, :, inner]
                term = jnp.dot(
                    weights[block].astype(jnp.bfloat16), value, preferred_element_type=jnp.float32
                )
                blended = term if blended is None else blended + term
            out_ref[:, cols] = (blended / total).astype(out_ref.dtype)

    def start(piece, _):
        send_own(piece)
        return 0

    lax.fori_loop(0, AHEAD, start, 0)
    activate()

    def step(t, _):
        @pl.when(t + AHEAD < PIECES)
        def _():
            send_own(t + AHEAD)

        @pl.when(t < PIECES)
        def _():
            pass_on(t, passed)
            pass_relayed(t)

        known = t - LAG

        @pl.when(within(known))
        def _():
            pass_on(known, passed_again)
            keep(known)

        @pl.when(t == 2)
        def _():
            edges_arrived()

        @pl.when((t >= 2) & (t < 5))
        def _():
            convolve(t - 2)

        @pl.when(t == 5)
        def _():
            decode()

        rising = known - HOP * z
        falling = known - HOP * (rows - 1 - z)
        final = known - HOP * (rows - 1)
        crossed = final - LAG
        ready = crossed - 1

        @pl.when(within(rising) & waves(rising))
        def _():
            @pl.when(z > 0)
            def _():
                wave(up_out, up_in, 4, rising, 4).wait_recv()

            @pl.when(z < rows - 1)
            def _():
                for part in range(2):
                    up_out[rising, part] = jnp.where(
                        group == z, mine(rising, part), up_in[rising, part]
                    )
                wave(up_out, up_in, 4, rising, 4).start()

        @pl.when(within(falling) & waves(falling))
        def _():
            @pl.when(z < rows - 1)
            def _():
                wave(down_out, down_in, 5, falling, -4).wait_recv()

            @pl.when(z > 0)
            def _():
                for part in range(2):
                    down_out[falling, part] = jnp.where(
                        group == z, mine(falling, part), down_in[falling, part]
                    )
                wave(down_out, down_in, 5, falling, -4).start()

        @pl.when(within(final) & waves(final))
        def _():
            for part in range(2):
                value = jnp.where(group < z, up_in[final, part], down_in[final, part])
                slots[3, final, part] = jnp.where(group == z, mine(final, part), value)

            @pl.when((role == 3) & crosses(final))
            def _():
                to_slot(slots.at[3, final], 3, final, 7, -3).start()

            @pl.when((role == 0) & crosses_back(final))
            def _():
                to_slot(slots.at[3, final], 3, final, 7, 3).start()

            @pl.when(role == 3)
            def _():
                to_slot(slots.at[3, final], 3, final, 6, -1).start()

            @pl.when(role == 0)
            def _():
                to_slot(slots.at[3, final], 3, final, 6, 1).start()

        @pl.when(within(crossed) & (role == 0) & crosses(crossed))
        def _():
            arrived(3, crossed)
            to_slot(slots.at[3, crossed], 3, crossed, 6, 1).start()

        @pl.when(within(crossed) & (role == 3) & crosses_back(crossed))
        def _():
            arrived(3, crossed)
            to_slot(slots.at[3, crossed], 3, crossed, 6, -1).start()

        @pl.when(within(ready))
        def _():
            @pl.when(role == 1)
            def _():
                for slot in range(3):
                    arrived(slot, ready)

            @pl.when((role == 1) | (role == 2))
            def _():
                arrived(3, ready)

            attend(ready)

        return 0

    lax.fori_loop(0, PIECES + 2 * LAG + 1 + HOP * (rows - 1), step, 0)

    def finish(piece, _):
        for which in range(4):

            @pl.when(role == which)
            def _():
                for slot, lane, offset in direct[which]:
                    to_slot(own(piece), slot, piece, lane, offset).wait_send()
                for slot, there, lane, offset in passed.get(which, ()) + passed_again.get(which, ()):
                    to_slot(slots.at[slot, piece], there, piece, lane, offset).wait_send()

        @pl.when(waves(piece) & (z < rows - 1))
        def _():
            wave(up_out, up_in, 4, piece, 4).wait_send()

        @pl.when(waves(piece) & (z > 0))
        def _():
            wave(down_out, down_in, 5, piece, -4).wait_send()

        @pl.when((role == 0) | (role == 3))
        def _():
            to_slot(slots.at[3, piece], 3, piece, 6, 1).wait_send()

        @pl.when(((role == 3) & crosses(piece)) | ((role == 0) & crosses_back(piece)))
        def _():
            to_slot(slots.at[3, piece], 3, piece, 7, -3).wait_send()

        @pl.when(role == 2)
        def _():
            to_relay(piece, 4).wait_send()

        @pl.when(relayed(piece))
        def _():
            to_slot(relay.at[piece], 1, piece, 8, 4).wait_send()

        return 0

    lax.fori_loop(0, PIECES, finish, 0)

    @pl.when(me < n - 1)
    def _():
        edge(0).wait_send()

    @pl.when(me > 0)
    def _():
        edge(1).wait_send()


def shards(
    queries,
    keys_values,
    owner,
    span_mask,
    lengths,
    frames,
    past_frames,
    norm_gain,
    conv_weight,
    conv_bias,
):
    n = lax.axis_size("span")
    rows, cols = queries.shape
    piece = (PIECES, 2, rows, cols // PIECES)
    frame_count, _, frame_cols, channels = frames.shape
    padded = -(-(frame_cols + 1) // 16) * 16
    attention_flops = 4 * rows * 5 * rows * cols
    conv_flops = 2 * frame_count * frame_cols * conv_weight.size
    scalars = pl.BlockSpec(memory_space=pltpu.SMEM)
    whole = pl.BlockSpec(memory_space=pltpu.VMEM)
    attended, decoded, limit = pl.pallas_call(
        functools.partial(block_kernel, n),
        out_shape=(
            jax.ShapeDtypeStruct((rows, cols), jnp.bfloat16),
            jax.ShapeDtypeStruct(frames.shape, jnp.bfloat16),
            jax.ShapeDtypeStruct((8, 128), jnp.int32),
        ),
        in_specs=[scalars] * 3 + [whole] * 6 + [pl.BlockSpec(memory_space=pl.ANY)],
        out_specs=(whole, whole, whole),
        scratch_shapes=[
            pltpu.VMEM((4,) + piece, jnp.bfloat16),
            pltpu.VMEM(piece, jnp.bfloat16),
            pltpu.VMEM(piece, jnp.bfloat16),
            pltpu.VMEM(piece, jnp.bfloat16),
            pltpu.VMEM(piece, jnp.bfloat16),
            pltpu.VMEM(piece, jnp.bfloat16),
            pltpu.VMEM((3, frame_count + past_frames.shape[0], padded, channels), jnp.bfloat16),
            pltpu.VMEM(conv_weight.shape, jnp.bfloat16),
            pltpu.VMEM((3, frame_count, padded + 16, channels), jnp.float32),
            pltpu.SemaphoreType.DMA((7, PIECES)),
            pltpu.SemaphoreType.DMA((9, PIECES)),
            pltpu.SemaphoreType.DMA((2,)),
            pltpu.SemaphoreType.DMA((2,)),
            pltpu.SemaphoreType.DMA,
        ],
        cost_estimate=pl.CostEstimate(
            flops=attention_flops + conv_flops,
            bytes_accessed=8 * rows * cols + 2 * conv_weight.size,
            transcendentals=5 * rows * rows * cols // DH,
        ),
        compiler_params=pltpu.CompilerParams(
            collective_id=0, has_side_effects=True, vmem_limit_bytes=60 * 1024 * 1024
        ),
        name="spans_and_decoder",
    )(
        owner,
        span_mask.T,
        lengths,
        queries,
        keys_values,
        frames,
        jnp.transpose(past_frames, (1, 2, 0, 3)),
        norm_gain,
        conv_bias,
        conv_weight,
    )
    row_ids = lax.broadcasted_iota(jnp.int32, (rows, 1), 0)
    return jnp.where(row_ids < limit[:1, :1], attended, 0.0).astype(jnp.bfloat16), decoded


def solution(mesh):
    placed = (
        P(("group", "span"), None),
        P(None, ("group", "span"), None),
        P("group"),
        P("group", None),
        P("group"),
        P("group", "span", None, None),
        P("group", "span", None, None),
        P(),
        P(),
        P(),
    )
    return jax.shard_map(
        shards,
        mesh=mesh,
        in_specs=placed,
        out_specs=(P(("group", "span"), None), P("group", "span", None, None)),
        check_vma=False,
    )
```

```python
import functools

import jax
import jax.numpy as jnp
from jax import lax
from jax.experimental import pallas as pl
from jax.experimental.pallas import tpu as pltpu
from jax.sharding import PartitionSpec as P

DH = 128
WIN = 4
PIECES = 20
AHEAD = 4
HOP = 2
LAG = 2
LOG2E = 1.4426950408889634
MESH = pl.DeviceIdType.MESH


def block_kernel(
    n,
    owner_ref,
    mask_ref,
    lengths_ref,
    q_ref,
    kv_ref,
    frames_ref,
    past_ref,
    gain_ref,
    shift_ref,
    weight_ref,
    out_ref,
    decoded_ref,
    slots,
    relay,
    sums,
    tops,
    totals,
    up_in,
    down_in,
    up_out,
    down_out,
    taps,
    weights_here,
    partial,
    recv,
    send,
    edge_recv,
    edge_send,
    weight_sem,
):
    tokens = q_ref.shape[0]
    frames, _, cols, channels = frames_ref.shape
    past = past_ref.shape[2]
    padded = taps.shape[2]
    rows = n // 4
    width = q_ref.shape[1] // PIECES
    me = lax.axis_index("span")
    role = lax.rem(me, 4)
    z = me // 4

    def at(offset):
        return lax.rem(me + offset + n, n)

    def columns(piece):
        return pl.ds(pl.multiple_of(piece * width, width), width)

    def own(piece):
        return kv_ref.at[:, :, columns(piece)]

    def to_slot(source, slot, piece, lane, offset):
        return pltpu.make_async_remote_copy(
            src_ref=source,
            dst_ref=slots.at[slot, piece],
            send_sem=send.at[lane, piece],
            recv_sem=recv.at[slot, piece],
            device_id={"span": at(offset)},
            device_id_type=MESH,
        )

    def wave(source, target, kind, piece, offset):
        return pltpu.make_async_remote_copy(
            src_ref=source.at[piece],
            dst_ref=target.at[piece],
            send_sem=send.at[kind, piece],
            recv_sem=recv.at[kind, piece],
            device_id={"span": at(offset)},
            device_id_type=MESH,
        )

    def arrived(slot, piece):
        to_slot(slots.at[slot, piece], slot, piece, 0, 1).wait_recv()

    def edge(which):
        return pltpu.make_async_remote_copy(
            src_ref=taps.at[1],
            dst_ref=taps.at[2 * which],
            send_sem=edge_send.at[which],
            recv_sem=edge_recv.at[which],
            device_id={"span": at(1 - 2 * which)},
            device_id_type=MESH,
        )

    weight_copy = pltpu.make_async_copy(weight_ref, weights_here, weight_sem)
    weight_copy.start()

    barrier = pltpu.get_barrier_semaphore()
    for offset in (-4, -3, -2, -1, 1, 2, 3, 4):
        pl.semaphore_signal(barrier, inc=1, device_id={"span": at(offset)}, device_id_type=MESH)
    pl.semaphore_wait(barrier, 8)

    direct = {
        0: ((1, 1, 2), (0, 0, 1)),
        1: ((2, 0, 3), (1, 1, 2)),
        2: ((0, 0, 1),),
        3: ((2, 0, 3),),
    }

    def even(piece):
        return lax.rem(piece, 2) == 0

    def to_relay(piece, offset):
        return pltpu.make_async_remote_copy(
            src_ref=own(piece),
            dst_ref=relay.at[piece],
            send_sem=send.at[1, piece],
            recv_sem=recv.at[6, piece],
            device_id={"span": at(offset)},
            device_id_type=MESH,
        )

    def relayed(piece):
        return ((role == 0) & even(piece)) | ((role == 2) & jnp.logical_not(even(piece)))

    def pass_relayed(piece):
        @pl.when(relayed(piece))
        def _():
            to_relay(piece, 1).wait_recv()

        @pl.when((role == 0) & even(piece))
        def _():
            to_slot(relay.at[piece], 1, piece, 8, 4).start()

        @pl.when((role == 2) & jnp.logical_not(even(piece)))
        def _():
            to_slot(relay.at[piece], 1, piece, 8, -2).start()

    def send_own(piece):
        @pl.when((role == 2) & even(piece))
        def _():
            to_relay(piece, -2).start()

        @pl.when((role == 2) & jnp.logical_not(even(piece)))
        def _():
            to_relay(piece, 4).start()

        for which, copies in direct.items():

            @pl.when(role == which)
            def _():
                for slot, lane, offset in copies:
                    to_slot(own(piece), slot, piece, lane, offset).start()

    passed = {2: ((2, 0, 2, -2), (1, 2, 3, 1)), 3: ((1, 0, 2, -1),)}
    passed_again = {0: ((1, 2, 2, 1), (0, 1, 3, 1))}
    kept = {0: (2,), 2: (0,), 3: (0, 2)}

    def pass_on(piece, table):
        for which, copies in table.items():

            @pl.when(role == which)
            def _():
                for slot, there, lane, offset in copies:
                    arrived(slot, piece)
                    to_slot(slots.at[slot, piece], there, piece, lane, offset).start()

    def keep(piece):
        for which, slots_here in kept.items():

            @pl.when(role == which)
            def _():
                for slot in slots_here:
                    arrived(slot, piece)

    anchor = owner_ref[0]
    behind = lax.rem(me - anchor + n, n)
    group = jnp.where(role == 0, lax.rem((anchor + 3) // 4, rows), anchor // 4)

    def mine(piece, part):
        value = jnp.where(behind == 2, slots[1, piece, part], slots[2, piece, part])
        value = jnp.where(behind == 1, slots[0, piece, part], value)
        return jnp.where(behind == 0, kv_ref[part, :, columns(piece)], value)

    def crosses(piece):
        return lax.rem(piece, 5) == 1

    def crosses_back(piece):
        return lax.rem(piece, 5) == 3

    def waves(piece):
        upper = (role == 3) & jnp.logical_not(crosses_back(piece))
        return upper | ((role == 0) & jnp.logical_not(crosses(piece)))

    def within(piece):
        return (piece >= 0) & (piece < PIECES)

    position = lax.rem(me - anchor - 1 + 2 * n, n)
    length = lengths_ref[me]
    limits = [length]
    for offset in range(1, WIN):
        allowed = (position >= offset) & (mask_ref[offset - 1, position] == 1)
        limits.append(jnp.where(allowed, lengths_ref[at(-offset)], 0))
    limits.append(jnp.where(behind == 0, 0, lengths_ref[anchor]))

    def activate():
        spare = partial.at[0, 0, 0:padded, :]
        for frame in range(past + frames):
            if frame < past:
                value = past_ref[0].astype(jnp.float32)[:, frame, :]
            else:
                value = frames_ref[frame - past, 0].astype(jnp.float32)
                squares = jnp.mean(value * value, axis=-1, keepdims=True)
                value = value * lax.rsqrt(squares + 1e-06) * gain_ref[...].reshape(1, channels)
                value = value / (1.0 + jnp.exp(-value))
            spare[...] = jnp.zeros(spare.shape, jnp.float32)
            spare[0:cols, :] = value
            taps[1, frame] = spare[...].astype(jnp.bfloat16)
        partial[0, :, 0:8, :] = jnp.zeros((frames, 8, channels), jnp.float32)

        @pl.when(me < n - 1)
        def _():
            edge(0).start()

        @pl.when(me > 0)
        def _():
            edge(1).start()

        @pl.when(me == 0)
        def _():
            taps[0] = jnp.zeros(taps.shape[1:], taps.dtype)

        @pl.when(me == n - 1)
        def _():
            taps[2] = jnp.zeros(taps.shape[1:], taps.dtype)

    def edges_arrived():
        @pl.when(me > 0)
        def _():
            edge(0).wait_recv()

        @pl.when(me < n - 1)
        def _():
            edge(1).wait_recv()

        weight_copy.wait()

    def convolve(col_tap):
        total = None
        for frame_tap in range(3):
            for row_tap in range(3):
                window_rows = taps[row_tap, frame_tap : frame_tap + frames]
                term = jnp.dot(
                    window_rows.reshape(frames * padded, channels),
                    weights_here[frame_tap, row_tap, col_tap],
                    preferred_element_type=jnp.float32,
                )
                total = term if total is None else total + term
        partial[col_tap, :, 8 : 8 + padded, :] = total.reshape(frames, padded, channels)

    def decode():
        for frame in range(frames):
            total = frames_ref[frame, 0].astype(jnp.float32) + shift_ref[...].reshape(1, channels)
            for col_tap in range(3):
                total = total + partial[col_tap, frame, 7 + col_tap : 7 + col_tap + cols, :]
            decoded_ref[frame, 0] = total.astype(decoded_ref.dtype)

    token = lax.broadcasted_iota(jnp.int32, (1, tokens), 1)
    row = lax.broadcasted_iota(jnp.int32, (tokens, 1), 0)

    def scores_of(piece, key, limit):
        score = lax.dot_general(
            q_ref[:, columns(piece)], key, (((1,), (1,)), ((), ())), preferred_element_type=jnp.float32
        )
        return score * (DH**-0.5 * LOG2E) + jnp.where(token < limit, 0.0, -1e30)

    def blend(weights, value):
        return jnp.dot(weights.astype(jnp.bfloat16), value, preferred_element_type=jnp.float32)

    def attend_window(piece):
        keys = [kv_ref[0, :, columns(piece)]] + [slots[slot, piece, 0] for slot in range(WIN - 1)]
        values = [kv_ref[1, :, columns(piece)]] + [slots[slot, piece, 1] for slot in range(WIN - 1)]
        scores = [scores_of(piece, key, limit) for key, limit in zip(keys, limits)]
        top = jnp.max(functools.reduce(jnp.maximum, scores), axis=-1, keepdims=True)
        weights = [jnp.exp2(score - top) for score in scores]
        total = jnp.sum(functools.reduce(jnp.add, weights), axis=-1, keepdims=True)
        blended = [blend(weight, value) for weight, value in zip(weights, values)]
        sums[piece] = functools.reduce(jnp.add, blended)
        tops[piece] = jnp.broadcast_to(top, tops.shape[1:])
        totals[piece] = jnp.broadcast_to(total, totals.shape[1:])

    def attend_anchor(piece):
        score = scores_of(piece, slots[3, piece, 0], limits[WIN])
        before = tops[piece]
        top = jnp.maximum(before, jnp.max(score, axis=-1, keepdims=True))
        weights = jnp.exp2(score - top[:, :1])
        scale = jnp.exp2(before - top)
        total = totals[piece] * scale + jnp.sum(weights, axis=-1, keepdims=True)
        blended = (sums[piece] * scale + blend(weights, slots[3, piece, 1])) / total
        out_ref[:, columns(piece)] = jnp.where(row < length, blended, 0.0).astype(out_ref.dtype)

    def start(piece, _):
        send_own(piece)
        return 0

    lax.fori_loop(0, AHEAD, start, 0)
    activate()

    def step(t, _):
        @pl.when(t + AHEAD < PIECES)
        def _():
            send_own(t + AHEAD)

        @pl.when(t < PIECES)
        def _():
            pass_on(t, passed)
            pass_relayed(t)

        known = t - LAG

        @pl.when(within(known))
        def _():
            pass_on(known, passed_again)
            keep(known)

        @pl.when(t == 2)
        def _():
            edges_arrived()

        @pl.when((t >= 2) & (t < 5))
        def _():
            convolve(t - 2)

        @pl.when(t == 5)
        def _():
            decode()

        rising = known - HOP * z
        falling = known - HOP * (rows - 1 - z)
        final = known - HOP * (rows - 1)
        crossed = final - LAG
        ready = crossed - 1

        @pl.when(within(rising) & waves(rising))
        def _():
            @pl.when(z > 0)
            def _():
                wave(up_out, up_in, 4, rising, 4).wait_recv()

            @pl.when(z < rows - 1)
            def _():
                for part in range(2):
                    up_out[rising, part] = jnp.where(
                        group == z, mine(rising, part), up_in[rising, part]
                    )
                wave(up_out, up_in, 4, rising, 4).start()

        @pl.when(within(falling) & waves(falling))
        def _():
            @pl.when(z < rows - 1)
            def _():
                wave(down_out, down_in, 5, falling, -4).wait_recv()

            @pl.when(z > 0)
            def _():
                for part in range(2):
                    down_out[falling, part] = jnp.where(
                        group == z, mine(falling, part), down_in[falling, part]
                    )
                wave(down_out, down_in, 5, falling, -4).start()

        @pl.when(within(final) & waves(final))
        def _():
            for part in range(2):
                value = jnp.where(group < z, up_in[final, part], down_in[final, part])
                slots[3, final, part] = jnp.where(group == z, mine(final, part), value)

            @pl.when((role == 3) & crosses(final))
            def _():
                to_slot(slots.at[3, final], 3, final, 7, -3).start()

            @pl.when((role == 0) & crosses_back(final))
            def _():
                to_slot(slots.at[3, final], 3, final, 7, 3).start()

            @pl.when(role == 3)
            def _():
                to_slot(slots.at[3, final], 3, final, 6, -1).start()

            @pl.when(role == 0)
            def _():
                to_slot(slots.at[3, final], 3, final, 6, 1).start()

        @pl.when(within(crossed) & (role == 0) & crosses(crossed))
        def _():
            arrived(3, crossed)
            to_slot(slots.at[3, crossed], 3, crossed, 6, 1).start()

        @pl.when(within(crossed) & (role == 3) & crosses_back(crossed))
        def _():
            arrived(3, crossed)
            to_slot(slots.at[3, crossed], 3, crossed, 6, -1).start()

        @pl.when(within(known - 1))
        def _():
            @pl.when(role == 1)
            def _():
                for slot in range(3):
                    arrived(slot, known - 1)

            attend_window(known - 1)

        @pl.when(within(ready))
        def _():
            @pl.when((role == 1) | (role == 2))
            def _():
                arrived(3, ready)

            attend_anchor(ready)

        return 0

    lax.fori_loop(0, PIECES + 2 * LAG + 1 + HOP * (rows - 1), step, 0)

    def finish(piece, _):
        for which in range(4):

            @pl.when(role == which)
            def _():
                for slot, lane, offset in direct[which]:
                    to_slot(own(piece), slot, piece, lane, offset).wait_send()
                for slot, there, lane, offset in passed.get(which, ()) + passed_again.get(which, ()):
                    to_slot(slots.at[slot, piece], there, piece, lane, offset).wait_send()

        @pl.when(waves(piece) & (z < rows - 1))
        def _():
            wave(up_out, up_in, 4, piece, 4).wait_send()

        @pl.when(waves(piece) & (z > 0))
        def _():
            wave(down_out, down_in, 5, piece, -4).wait_send()

        @pl.when((role == 0) | (role == 3))
        def _():
            to_slot(slots.at[3, piece], 3, piece, 6, 1).wait_send()

        @pl.when(((role == 3) & crosses(piece)) | ((role == 0) & crosses_back(piece)))
        def _():
            to_slot(slots.at[3, piece], 3, piece, 7, -3).wait_send()

        @pl.when(role == 2)
        def _():
            to_relay(piece, 4).wait_send()

        @pl.when(relayed(piece))
        def _():
            to_slot(relay.at[piece], 1, piece, 8, 4).wait_send()

        return 0

    lax.fori_loop(0, PIECES, finish, 0)

    @pl.when(me < n - 1)
    def _():
        edge(0).wait_send()

    @pl.when(me > 0)
    def _():
        edge(1).wait_send()


def shards(
    queries,
    keys_values,
    owner,
    span_mask,
    lengths,
    frames,
    past_frames,
    norm_gain,
    conv_weight,
    conv_bias,
):
    n = lax.axis_size("span")
    rows, cols = queries.shape
    piece = (PIECES, 2, rows, cols // PIECES)
    frame_count, _, frame_cols, channels = frames.shape
    padded = -(-(frame_cols + 1) // 16) * 16
    attention_flops = 4 * rows * 5 * rows * cols
    conv_flops = 2 * frame_count * frame_cols * conv_weight.size
    scalars = pl.BlockSpec(memory_space=pltpu.SMEM)
    whole = pl.BlockSpec(memory_space=pltpu.VMEM)
    return pl.pallas_call(
        functools.partial(block_kernel, n),
        out_shape=(
            jax.ShapeDtypeStruct((rows, cols), jnp.bfloat16),
            jax.ShapeDtypeStruct(frames.shape, jnp.bfloat16),
        ),
        in_specs=[scalars] * 3 + [whole] * 6 + [pl.BlockSpec(memory_space=pl.ANY)],
        out_specs=(whole, whole),
        scratch_shapes=[
            pltpu.VMEM((4,) + piece, jnp.bfloat16),
            pltpu.VMEM(piece, jnp.bfloat16),
            pltpu.VMEM((PIECES, rows, DH), jnp.float32),
            pltpu.VMEM((PIECES, rows, DH), jnp.float32),
            pltpu.VMEM((PIECES, rows, DH), jnp.float32),
            pltpu.VMEM(piece, jnp.bfloat16),
            pltpu.VMEM(piece, jnp.bfloat16),
            pltpu.VMEM(piece, jnp.bfloat16),
            pltpu.VMEM(piece, jnp.bfloat16),
            pltpu.VMEM((3, frame_count + past_frames.shape[0], padded, channels), jnp.bfloat16),
            pltpu.VMEM(conv_weight.shape, jnp.bfloat16),
            pltpu.VMEM((3, frame_count, padded + 16, channels), jnp.float32),
            pltpu.SemaphoreType.DMA((7, PIECES)),
            pltpu.SemaphoreType.DMA((9, PIECES)),
            pltpu.SemaphoreType.DMA((2,)),
            pltpu.SemaphoreType.DMA((2,)),
            pltpu.SemaphoreType.DMA,
        ],
        cost_estimate=pl.CostEstimate(
            flops=attention_flops + conv_flops,
            bytes_accessed=8 * rows * cols + 2 * conv_weight.size,
            transcendentals=5 * rows * rows * cols // DH,
        ),
        compiler_params=pltpu.CompilerParams(
            collective_id=0, has_side_effects=True, vmem_limit_bytes=60 * 1024 * 1024
        ),
        name="spans_and_decoder",
    )(
        owner,
        span_mask.T,
        lengths,
        queries,
        keys_values,
        frames,
        jnp.transpose(past_frames, (1, 2, 0, 3)),
        norm_gain,
        conv_bias,
        conv_weight,
    )


def solution(mesh):
    placed = (
        P(("group", "span"), None),
        P(None, ("group", "span"), None),
        P("group"),
        P("group", None),
        P("group"),
        P("group", "span", None, None),
        P("group", "span", None, None),
        P(),
        P(),
        P(),
    )
    return jax.shard_map(
        shards,
        mesh=mesh,
        in_specs=placed,
        out_specs=(P(("group", "span"), None), P("group", "span", None, None)),
        check_vma=False,
    )
```

```python
import functools

import jax
import jax.numpy as jnp
from jax import lax
from jax.experimental import pallas as pl
from jax.experimental.pallas import tpu as pltpu
from jax.sharding import PartitionSpec as P

DH = 128
WIN = 4
PIECES = 20
AHEAD = 4
HOP = 2
LAG = 2
LOG2E = 1.4426950408889634
MESH = pl.DeviceIdType.MESH


def block_kernel(
    n,
    owner_ref,
    mask_ref,
    lengths_ref,
    q_ref,
    kv_ref,
    frames_ref,
    past_ref,
    gain_ref,
    shift_ref,
    weight_ref,
    out_ref,
    decoded_ref,
    slots,
    relay,
    sums,
    tops,
    totals,
    up_in,
    down_in,
    up_out,
    down_out,
    taps,
    weights_here,
    partial,
    recv,
    send,
    edge_recv,
    edge_send,
    weight_sem,
):
    tokens = q_ref.shape[0]
    frames, _, cols, channels = frames_ref.shape
    past = past_ref.shape[2]
    padded = taps.shape[2]
    rows = n // 4
    width = q_ref.shape[1] // PIECES
    me = lax.axis_index("span")
    role = lax.rem(me, 4)
    z = me // 4

    def at(offset):
        return lax.rem(me + offset + n, n)

    def columns(piece):
        return pl.ds(pl.multiple_of(piece * width, width), width)

    def own(piece):
        return kv_ref.at[:, :, columns(piece)]

    def to_slot(source, slot, piece, lane, offset):
        return pltpu.make_async_remote_copy(
            src_ref=source,
            dst_ref=slots.at[slot, piece],
            send_sem=send.at[lane, piece],
            recv_sem=recv.at[slot, piece],
            device_id={"span": at(offset)},
            device_id_type=MESH,
        )

    def wave(source, target, kind, piece, offset):
        return pltpu.make_async_remote_copy(
            src_ref=source.at[piece],
            dst_ref=target.at[piece],
            send_sem=send.at[kind, piece],
            recv_sem=recv.at[kind, piece],
            device_id={"span": at(offset)},
            device_id_type=MESH,
        )

    def arrived(slot, piece):
        to_slot(slots.at[slot, piece], slot, piece, 0, 1).wait_recv()

    def edge(which):
        return pltpu.make_async_remote_copy(
            src_ref=taps.at[1],
            dst_ref=taps.at[2 * which],
            send_sem=edge_send.at[which],
            recv_sem=edge_recv.at[which],
            device_id={"span": at(1 - 2 * which)},
            device_id_type=MESH,
        )

    weight_copy = pltpu.make_async_copy(weight_ref, weights_here, weight_sem)
    weight_copy.start()

    barrier = pltpu.get_barrier_semaphore()
    for offset in (-4, -3, -2, -1, 1, 2, 3, 4):
        pl.semaphore_signal(barrier, inc=1, device_id={"span": at(offset)}, device_id_type=MESH)
    pl.semaphore_wait(barrier, 8)

    direct = {
        0: ((1, 1, 2), (0, 0, 1)),
        1: ((2, 0, 3), (1, 1, 2)),
        2: ((0, 0, 1),),
        3: ((2, 0, 3),),
    }

    def even(piece):
        return lax.rem(piece, 2) == 0

    def to_relay(piece, offset):
        return pltpu.make_async_remote_copy(
            src_ref=own(piece),
            dst_ref=relay.at[piece],
            send_sem=send.at[1, piece],
            recv_sem=recv.at[6, piece],
            device_id={"span": at(offset)},
            device_id_type=MESH,
        )

    def relayed(piece):
        return ((role == 0) & even(piece)) | ((role == 2) & jnp.logical_not(even(piece)))

    def pass_relayed(piece):
        @pl.when(relayed(piece))
        def _():
            to_relay(piece, 1).wait_recv()

        @pl.when((role == 0) & even(piece))
        def _():
            to_slot(relay.at[piece], 1, piece, 8, 4).start()

        @pl.when((role == 2) & jnp.logical_not(even(piece)))
        def _():
            to_slot(relay.at[piece], 1, piece, 8, -2).start()

    def send_own(piece):
        @pl.when((role == 2) & even(piece))
        def _():
            to_relay(piece, -2).start()

        @pl.when((role == 2) & jnp.logical_not(even(piece)))
        def _():
            to_relay(piece, 4).start()

        for which, copies in direct.items():

            @pl.when(role == which)
            def _():
                for slot, lane, offset in copies:
                    to_slot(own(piece), slot, piece, lane, offset).start()

    passed = {2: ((2, 0, 2, -2), (1, 2, 3, 1)), 3: ((1, 0, 2, -1),)}
    passed_again = {0: ((1, 2, 2, 1), (0, 1, 3, 1))}
    kept = {0: (2,), 2: (0,), 3: (0, 2)}

    def pass_on(piece, table):
        for which, copies in table.items():

            @pl.when(role == which)
            def _():
                for slot, there, lane, offset in copies:
                    arrived(slot, piece)
                    to_slot(slots.at[slot, piece], there, piece, lane, offset).start()

    def keep(piece):
        for which, slots_here in kept.items():

            @pl.when(role == which)
            def _():
                for slot in slots_here:
                    arrived(slot, piece)

    anchor = owner_ref[0]
    behind = lax.rem(me - anchor + n, n)
    group = jnp.where(role == 1, lax.rem((anchor + 2) // 4, rows), anchor // 4)

    def mine(piece, part):
        value = jnp.where(behind == 2, slots[1, piece, part], slots[2, piece, part])
        value = jnp.where(behind == 1, slots[0, piece, part], value)
        return jnp.where(behind == 0, kv_ref[part, :, columns(piece)], value)

    def crosses(piece):
        return lax.rem(piece, 5) == 1

    def crosses_back(piece):
        return lax.rem(piece, 5) == 3

    def waves(piece):
        upper = (role == 3) & jnp.logical_not(crosses_back(piece))
        return upper | ((role == 1) & jnp.logical_not(crosses(piece)))

    def within(piece):
        return (piece >= 0) & (piece < PIECES)

    position = lax.rem(me - anchor - 1 + 2 * n, n)
    length = lengths_ref[me]
    limits = [length]
    for offset in range(1, WIN):
        allowed = (position >= offset) & (mask_ref[offset - 1, position] == 1)
        limits.append(jnp.where(allowed, lengths_ref[at(-offset)], 0))
    limits.append(jnp.where(behind == 0, 0, lengths_ref[anchor]))

    def activate():
        spare = partial.at[0, 0, 0:padded, :]
        for frame in range(past + frames):
            if frame < past:
                value = past_ref[0].astype(jnp.float32)[:, frame, :]
            else:
                value = frames_ref[frame - past, 0].astype(jnp.float32)
                squares = jnp.mean(value * value, axis=-1, keepdims=True)
                value = value * lax.rsqrt(squares + 1e-06) * gain_ref[...].reshape(1, channels)
                value = value / (1.0 + jnp.exp(-value))
            spare[...] = jnp.zeros(spare.shape, jnp.float32)
            spare[0:cols, :] = value
            taps[1, frame] = spare[...].astype(jnp.bfloat16)
        partial[0, :, 0:8, :] = jnp.zeros((frames, 8, channels), jnp.float32)

        @pl.when(me < n - 1)
        def _():
            edge(0).start()

        @pl.when(me > 0)
        def _():
            edge(1).start()

        @pl.when(me == 0)
        def _():
            taps[0] = jnp.zeros(taps.shape[1:], taps.dtype)

        @pl.when(me == n - 1)
        def _():
            taps[2] = jnp.zeros(taps.shape[1:], taps.dtype)

    def edges_arrived():
        @pl.when(me > 0)
        def _():
            edge(0).wait_recv()

        @pl.when(me < n - 1)
        def _():
            edge(1).wait_recv()

        weight_copy.wait()

    def convolve(col_tap):
        total = None
        for frame_tap in range(3):
            for row_tap in range(3):
                window_rows = taps[row_tap, frame_tap : frame_tap + frames]
                term = jnp.dot(
                    window_rows.reshape(frames * padded, channels),
                    weights_here[frame_tap, row_tap, col_tap],
                    preferred_element_type=jnp.float32,
                )
                total = term if total is None else total + term
        partial[col_tap, :, 8 : 8 + padded, :] = total.reshape(frames, padded, channels)

    def decode():
        for frame in range(frames):
            total = frames_ref[frame, 0].astype(jnp.float32) + shift_ref[...].reshape(1, channels)
            for col_tap in range(3):
                total = total + partial[col_tap, frame, 7 + col_tap : 7 + col_tap + cols, :]
            decoded_ref[frame, 0] = total.astype(decoded_ref.dtype)

    token = lax.broadcasted_iota(jnp.int32, (1, tokens), 1)
    row = lax.broadcasted_iota(jnp.int32, (tokens, 1), 0)

    def scores_of(piece, key, limit):
        score = lax.dot_general(
            q_ref[:, columns(piece)], key, (((1,), (1,)), ((), ())), preferred_element_type=jnp.float32
        )
        return score * (DH**-0.5 * LOG2E) + jnp.where(token < limit, 0.0, -1e30)

    def blend(weights, value):
        return jnp.dot(weights.astype(jnp.bfloat16), value, preferred_element_type=jnp.float32)

    def attend_window(piece):
        keys = [kv_ref[0, :, columns(piece)]] + [slots[slot, piece, 0] for slot in range(WIN - 1)]
        values = [kv_ref[1, :, columns(piece)]] + [slots[slot, piece, 1] for slot in range(WIN - 1)]
        scores = [scores_of(piece, key, limit) for key, limit in zip(keys, limits)]
        top = jnp.max(functools.reduce(jnp.maximum, scores), axis=-1, keepdims=True)
        weights = [jnp.exp2(score - top) for score in scores]
        total = jnp.sum(functools.reduce(jnp.add, weights), axis=-1, keepdims=True)
        blended = [blend(weight, value) for weight, value in zip(weights, values)]
        sums[piece] = functools.reduce(jnp.add, blended)
        tops[piece] = jnp.broadcast_to(top, tops.shape[1:])
        totals[piece] = jnp.broadcast_to(total, totals.shape[1:])

    def attend_anchor(piece):
        score = scores_of(piece, slots[3, piece, 0], limits[WIN])
        before = tops[piece]
        top = jnp.maximum(before, jnp.max(score, axis=-1, keepdims=True))
        weights = jnp.exp2(score - top[:, :1])
        scale = jnp.exp2(before - top)
        total = totals[piece] * scale + jnp.sum(weights, axis=-1, keepdims=True)
        blended = (sums[piece] * scale + blend(weights, slots[3, piece, 1])) / total
        out_ref[:, columns(piece)] = jnp.where(row < length, blended, 0.0).astype(out_ref.dtype)

    def start(piece, _):
        send_own(piece)
        return 0

    lax.fori_loop(0, AHEAD, start, 0)
    activate()

    def step(t, _):
        @pl.when(t + AHEAD < PIECES)
        def _():
            send_own(t + AHEAD)

        @pl.when(t < PIECES)
        def _():
            pass_on(t, passed)
            pass_relayed(t)

        known = t - LAG

        @pl.when(within(known))
        def _():
            pass_on(known, passed_again)
            keep(known)

        @pl.when(t == 2)
        def _():
            edges_arrived()

        @pl.when((t >= 2) & (t < 5))
        def _():
            convolve(t - 2)

        @pl.when(t == 5)
        def _():
            decode()

        settled = known - 1

        @pl.when(within(settled) & (role == 1))
        def _():
            for slot in range(3):
                arrived(slot, settled)

        rising = settled - HOP * z
        falling = settled - HOP * (rows - 1 - z)
        final = settled - HOP * (rows - 1)
        crossed = final - LAG
        ready = crossed - 1

        @pl.when(within(rising) & waves(rising))
        def _():
            @pl.when(z > 0)
            def _():
                wave(up_out, up_in, 4, rising, 4).wait_recv()

            @pl.when(z < rows - 1)
            def _():
                for part in range(2):
                    up_out[rising, part] = jnp.where(
                        group == z, mine(rising, part), up_in[rising, part]
                    )
                wave(up_out, up_in, 4, rising, 4).start()

        @pl.when(within(falling) & waves(falling))
        def _():
            @pl.when(z < rows - 1)
            def _():
                wave(down_out, down_in, 5, falling, -4).wait_recv()

            @pl.when(z > 0)
            def _():
                for part in range(2):
                    down_out[falling, part] = jnp.where(
                        group == z, mine(falling, part), down_in[falling, part]
                    )
                wave(down_out, down_in, 5, falling, -4).start()

        @pl.when(within(final) & waves(final))
        def _():
            for part in range(2):
                value = jnp.where(group < z, up_in[final, part], down_in[final, part])
                slots[3, final, part] = jnp.where(group == z, mine(final, part), value)

            @pl.when((role == 3) & crosses(final))
            def _():
                to_slot(slots.at[3, final], 3, final, 7, -2).start()

            @pl.when((role == 1) & crosses_back(final))
            def _():
                to_slot(slots.at[3, final], 3, final, 7, 2).start()

            to_slot(slots.at[3, final], 3, final, 6, -1).start()

        @pl.when(within(crossed))
        def _():
            @pl.when(((role == 1) & crosses(crossed)) | ((role == 3) & crosses_back(crossed)))
            def _():
                arrived(3, crossed)
                to_slot(slots.at[3, crossed], 3, crossed, 6, -1).start()

        @pl.when(within(settled))
        def _():
            attend_window(settled)

        @pl.when(within(ready))
        def _():
            @pl.when((role == 0) | (role == 2))
            def _():
                arrived(3, ready)

            attend_anchor(ready)

        return 0

    lax.fori_loop(0, PIECES + 2 * LAG + 2 + HOP * (rows - 1), step, 0)

    def finish(piece, _):
        for which in range(4):

            @pl.when(role == which)
            def _():
                for slot, lane, offset in direct[which]:
                    to_slot(own(piece), slot, piece, lane, offset).wait_send()
                for slot, there, lane, offset in passed.get(which, ()) + passed_again.get(which, ()):
                    to_slot(slots.at[slot, piece], there, piece, lane, offset).wait_send()

        @pl.when(waves(piece) & (z < rows - 1))
        def _():
            wave(up_out, up_in, 4, piece, 4).wait_send()

        @pl.when(waves(piece) & (z > 0))
        def _():
            wave(down_out, down_in, 5, piece, -4).wait_send()

        @pl.when((role == 1) | (role == 3))
        def _():
            to_slot(slots.at[3, piece], 3, piece, 6, -1).wait_send()

        @pl.when(((role == 3) & crosses(piece)) | ((role == 1) & crosses_back(piece)))
        def _():
            to_slot(slots.at[3, piece], 3, piece, 7, -3).wait_send()

        @pl.when(role == 2)
        def _():
            to_relay(piece, 4).wait_send()

        @pl.when(relayed(piece))
        def _():
            to_slot(relay.at[piece], 1, piece, 8, 4).wait_send()

        return 0

    lax.fori_loop(0, PIECES, finish, 0)

    @pl.when(me < n - 1)
    def _():
        edge(0).wait_send()

    @pl.when(me > 0)
    def _():
        edge(1).wait_send()


def shards(
    queries,
    keys_values,
    owner,
    span_mask,
    lengths,
    frames,
    past_frames,
    norm_gain,
    conv_weight,
    conv_bias,
):
    n = lax.axis_size("span")
    rows, cols = queries.shape
    piece = (PIECES, 2, rows, cols // PIECES)
    frame_count, _, frame_cols, channels = frames.shape
    padded = -(-(frame_cols + 1) // 16) * 16
    attention_flops = 4 * rows * 5 * rows * cols
    conv_flops = 2 * frame_count * frame_cols * conv_weight.size
    scalars = pl.BlockSpec(memory_space=pltpu.SMEM)
    whole = pl.BlockSpec(memory_space=pltpu.VMEM)
    return pl.pallas_call(
        functools.partial(block_kernel, n),
        out_shape=(
            jax.ShapeDtypeStruct((rows, cols), jnp.bfloat16),
            jax.ShapeDtypeStruct(frames.shape, jnp.bfloat16),
        ),
        in_specs=[scalars] * 3 + [whole] * 6 + [pl.BlockSpec(memory_space=pl.ANY)],
        out_specs=(whole, whole),
        scratch_shapes=[
            pltpu.VMEM((4,) + piece, jnp.bfloat16),
            pltpu.VMEM(piece, jnp.bfloat16),
            pltpu.VMEM((PIECES, rows, DH), jnp.float32),
            pltpu.VMEM((PIECES, rows, DH), jnp.float32),
            pltpu.VMEM((PIECES, rows, DH), jnp.float32),
            pltpu.VMEM(piece, jnp.bfloat16),
            pltpu.VMEM(piece, jnp.bfloat16),
            pltpu.VMEM(piece, jnp.bfloat16),
            pltpu.VMEM(piece, jnp.bfloat16),
            pltpu.VMEM((3, frame_count + past_frames.shape[0], padded, channels), jnp.bfloat16),
            pltpu.VMEM(conv_weight.shape, jnp.bfloat16),
            pltpu.VMEM((3, frame_count, padded + 16, channels), jnp.float32),
            pltpu.SemaphoreType.DMA((7, PIECES)),
            pltpu.SemaphoreType.DMA((9, PIECES)),
            pltpu.SemaphoreType.DMA((2,)),
            pltpu.SemaphoreType.DMA((2,)),
            pltpu.SemaphoreType.DMA,
        ],
        cost_estimate=pl.CostEstimate(
            flops=attention_flops + conv_flops,
            bytes_accessed=8 * rows * cols + 2 * conv_weight.size,
            transcendentals=5 * rows * rows * cols // DH,
        ),
        compiler_params=pltpu.CompilerParams(
            collective_id=0, has_side_effects=True, vmem_limit_bytes=60 * 1024 * 1024
        ),
        name="spans_and_decoder",
    )(
        owner,
        span_mask.T,
        lengths,
        queries,
        keys_values,
        frames,
        jnp.transpose(past_frames, (1, 2, 0, 3)),
        norm_gain,
        conv_bias,
        conv_weight,
    )


def solution(mesh):
    placed = (
        P(("group", "span"), None),
        P(None, ("group", "span"), None),
        P("group"),
        P("group", None),
        P("group"),
        P("group", "span", None, None),
        P("group", "span", None, None),
        P(),
        P(),
        P(),
    )
    return jax.shard_map(
        shards,
        mesh=mesh,
        in_specs=placed,
        out_specs=(P(("group", "span"), None), P("group", "span", None, None)),
        check_vma=False,
    )
```

```python
import functools

import jax
import jax.numpy as jnp
from jax import lax
from jax.experimental import pallas as pl
from jax.experimental.pallas import tpu as pltpu
from jax.sharding import PartitionSpec as P

DH = 128
WIN = 4
PIECES = 20
AHEAD = 4
HOP = 2
LAG = 2
LOG2E = 1.4426950408889634
MESH = pl.DeviceIdType.MESH


def block_kernel(
    n,
    owner_ref,
    mask_ref,
    lengths_ref,
    q_ref,
    kv_ref,
    frames_ref,
    past_ref,
    gain_ref,
    shift_ref,
    weight_ref,
    out_ref,
    decoded_ref,
    slots,
    relay,
    sums,
    tops,
    totals,
    up_in,
    down_in,
    up_out,
    down_out,
    taps,
    weights_here,
    partial,
    recv,
    send,
    edge_recv,
    edge_send,
    weight_sem,
):
    tokens = q_ref.shape[0]
    frames, _, cols, channels = frames_ref.shape
    past = past_ref.shape[2]
    padded = taps.shape[2]
    rows = n // 4
    width = q_ref.shape[1] // PIECES
    me = lax.axis_index("span")
    role = lax.rem(me, 4)
    z = me // 4

    def at(offset):
        return lax.rem(me + offset + n, n)

    def columns(piece):
        return pl.ds(pl.multiple_of(piece * width, width), width)

    def own(piece):
        return kv_ref.at[:, :, columns(piece)]

    def to_slot(source, slot, piece, lane, offset):
        return pltpu.make_async_remote_copy(
            src_ref=source,
            dst_ref=slots.at[slot, piece],
            send_sem=send.at[lane, piece],
            recv_sem=recv.at[slot, piece],
            device_id={"span": at(offset)},
            device_id_type=MESH,
        )

    def wave(source, target, kind, piece, offset):
        return pltpu.make_async_remote_copy(
            src_ref=source.at[piece],
            dst_ref=target.at[piece],
            send_sem=send.at[kind, piece],
            recv_sem=recv.at[kind, piece],
            device_id={"span": at(offset)},
            device_id_type=MESH,
        )

    def arrived(slot, piece):
        to_slot(slots.at[slot, piece], slot, piece, 0, 1).wait_recv()

    def edge(which):
        return pltpu.make_async_remote_copy(
            src_ref=taps.at[1],
            dst_ref=taps.at[2 * which],
            send_sem=edge_send.at[which],
            recv_sem=edge_recv.at[which],
            device_id={"span": at(1 - 2 * which)},
            device_id_type=MESH,
        )

    weight_copy = pltpu.make_async_copy(weight_ref, weights_here, weight_sem)
    weight_copy.start()

    barrier = pltpu.get_barrier_semaphore()
    for offset in (-4, -3, -2, -1, 1, 2, 3, 4):
        pl.semaphore_signal(barrier, inc=1, device_id={"span": at(offset)}, device_id_type=MESH)
    pl.semaphore_wait(barrier, 8)

    direct = {
        0: ((1, 1, 2), (0, 0, 1)),
        1: ((2, 0, 3), (1, 1, 2)),
        2: ((0, 0, 1),),
        3: ((2, 0, 3),),
    }

    def even(piece):
        return lax.rem(piece, 2) == 0

    def to_relay(piece, offset):
        return pltpu.make_async_remote_copy(
            src_ref=own(piece),
            dst_ref=relay.at[piece],
            send_sem=send.at[1, piece],
            recv_sem=recv.at[6, piece],
            device_id={"span": at(offset)},
            device_id_type=MESH,
        )

    def relayed(piece):
        return ((role == 0) & even(piece)) | ((role == 2) & jnp.logical_not(even(piece)))

    def pass_relayed(piece):
        @pl.when(relayed(piece))
        def _():
            to_relay(piece, 1).wait_recv()

        @pl.when((role == 0) & even(piece))
        def _():
            to_slot(relay.at[piece], 1, piece, 8, 4).start()

        @pl.when((role == 2) & jnp.logical_not(even(piece)))
        def _():
            to_slot(relay.at[piece], 1, piece, 8, -2).start()

    def send_own(piece):
        @pl.when((role == 2) & even(piece))
        def _():
            to_relay(piece, -2).start()

        @pl.when((role == 2) & jnp.logical_not(even(piece)))
        def _():
            to_relay(piece, 4).start()

        for which, copies in direct.items():

            @pl.when(role == which)
            def _():
                for slot, lane, offset in copies:
                    to_slot(own(piece), slot, piece, lane, offset).start()

    passed = {2: ((2, 0, 2, -2), (1, 2, 3, 1)), 3: ((1, 0, 2, -1),)}
    passed_again = {0: ((1, 2, 2, 1), (0, 1, 3, 1))}
    kept = {0: (2,), 2: (0,), 3: (0, 2)}

    def pass_on(piece, table):
        for which, copies in table.items():

            @pl.when(role == which)
            def _():
                for slot, there, lane, offset in copies:
                    arrived(slot, piece)
                    to_slot(slots.at[slot, piece], there, piece, lane, offset).start()

    def keep(piece):
        for which, slots_here in kept.items():

            @pl.when(role == which)
            def _():
                for slot in slots_here:
                    arrived(slot, piece)

    anchor = owner_ref[0]
    behind = lax.rem(me - anchor + n, n)
    group = jnp.where(role == 1, lax.rem((anchor + 2) // 4, rows), anchor // 4)

    def mine(piece, part):
        value = jnp.where(behind == 2, slots[1, piece, part], slots[2, piece, part])
        value = jnp.where(behind == 1, slots[0, piece, part], value)
        return jnp.where(behind == 0, kv_ref[part, :, columns(piece)], value)

    def crosses(piece):
        return lax.rem(piece, 5) == 1

    def crosses_back(piece):
        return lax.rem(piece, 5) == 3

    def waves(piece):
        upper = (role == 3) & jnp.logical_not(crosses_back(piece))
        return upper | ((role == 1) & jnp.logical_not(crosses(piece)))

    def within(piece):
        return (piece >= 0) & (piece < PIECES)

    position = lax.rem(me - anchor - 1 + 2 * n, n)
    length = lengths_ref[me]
    limits = [length]
    for offset in range(1, WIN):
        allowed = (position >= offset) & (mask_ref[offset - 1, position] == 1)
        limits.append(jnp.where(allowed, lengths_ref[at(-offset)], 0))
    limits.append(jnp.where(behind == 0, 0, lengths_ref[anchor]))

    def activate():
        spare = partial.at[0, 0, 0:padded, :]
        for frame in range(past + frames):
            if frame < past:
                value = past_ref[0].astype(jnp.float32)[:, frame, :]
            else:
                value = frames_ref[frame - past, 0].astype(jnp.float32)
                squares = jnp.mean(value * value, axis=-1, keepdims=True)
                value = value * lax.rsqrt(squares + 1e-06) * gain_ref[...].reshape(1, channels)
                value = value / (1.0 + jnp.exp(-value))
            spare[...] = jnp.zeros(spare.shape, jnp.float32)
            spare[0:cols, :] = value
            taps[1, frame] = spare[...].astype(jnp.bfloat16)
        partial[0, :, 0:8, :] = jnp.zeros((frames, 8, channels), jnp.float32)

        @pl.when(me < n - 1)
        def _():
            edge(0).start()

        @pl.when(me > 0)
        def _():
            edge(1).start()

        @pl.when(me == 0)
        def _():
            taps[0] = jnp.zeros(taps.shape[1:], taps.dtype)

        @pl.when(me == n - 1)
        def _():
            taps[2] = jnp.zeros(taps.shape[1:], taps.dtype)

    def edges_arrived():
        @pl.when(me > 0)
        def _():
            edge(0).wait_recv()

        @pl.when(me < n - 1)
        def _():
            edge(1).wait_recv()

        weight_copy.wait()

    def convolve(col_tap):
        total = None
        for frame_tap in range(3):
            for row_tap in range(3):
                window_rows = taps[row_tap, frame_tap : frame_tap + frames]
                term = jnp.dot(
                    window_rows.reshape(frames * padded, channels),
                    weights_here[frame_tap, row_tap, col_tap],
                    preferred_element_type=jnp.float32,
                )
                total = term if total is None else total + term
        partial[col_tap, :, 8 : 8 + padded, :] = total.reshape(frames, padded, channels)

    def decode():
        for frame in range(frames):
            total = frames_ref[frame, 0].astype(jnp.float32) + shift_ref[...].reshape(1, channels)
            for col_tap in range(3):
                total = total + partial[col_tap, frame, 7 + col_tap : 7 + col_tap + cols, :]
            decoded_ref[frame, 0] = total.astype(decoded_ref.dtype)

    token = lax.broadcasted_iota(jnp.int32, (1, tokens), 1)
    row = lax.broadcasted_iota(jnp.int32, (tokens, 1), 0)

    def scores_of(piece, key, limit):
        score = lax.dot_general(
            q_ref[:, columns(piece)], key, (((1,), (1,)), ((), ())), preferred_element_type=jnp.float32
        )
        return score * (DH**-0.5 * LOG2E) + jnp.where(token < limit, 0.0, -1e30)

    def blend(weights, value):
        wide = jnp.concatenate([value, jnp.ones_like(value)], axis=1)
        return jnp.dot(weights.astype(jnp.bfloat16), wide, preferred_element_type=jnp.float32)

    def attend_window(pieces):
        scores = []
        for piece in pieces:
            keys = [kv_ref[0, :, columns(piece)]] + [slots[slot, piece, 0] for slot in range(WIN - 1)]
            scores.append([scores_of(piece, key, limit) for key, limit in zip(keys, limits)])
        for which, piece in enumerate(pieces):
            values = [kv_ref[1, :, columns(piece)]] + [slots[slot, piece, 1] for slot in range(WIN - 1)]
            top = jnp.max(functools.reduce(jnp.maximum, scores[which]), axis=-1, keepdims=True)
            blended = [
                blend(jnp.exp2(score - top), value) for score, value in zip(scores[which], values)
            ]
            blended = functools.reduce(jnp.add, blended)
            sums[piece] = blended[:, :DH]
            totals[piece] = blended[:, DH:]
            tops[piece] = jnp.broadcast_to(top, tops.shape[1:])

    def attend_anchor(pieces):
        scores = [scores_of(piece, slots[3, piece, 0], limits[WIN]) for piece in pieces]
        for score, piece in zip(scores, pieces):
            before = tops[piece]
            top = jnp.maximum(before, jnp.max(score, axis=-1, keepdims=True))
            added = blend(jnp.exp2(score - top[:, :1]), slots[3, piece, 1])
            scale = jnp.exp2(before - top)
            total = totals[piece] * scale + added[:, DH:]
            blended = (sums[piece] * scale + added[:, :DH]) / total
            out_ref[:, columns(piece)] = jnp.where(row < length, blended, 0.0).astype(out_ref.dtype)

    def pair_ends(piece):
        return within(piece) & (lax.rem(piece, 2) == 1)

    def start(piece, _):
        send_own(piece)
        return 0

    lax.fori_loop(0, AHEAD, start, 0)
    activate()

    def step(t, _):
        @pl.when(t + AHEAD < PIECES)
        def _():
            send_own(t + AHEAD)

        @pl.when(t < PIECES)
        def _():
            pass_on(t, passed)
            pass_relayed(t)

        known = t - LAG

        @pl.when(within(known))
        def _():
            pass_on(known, passed_again)
            keep(known)

        @pl.when(t == 2)
        def _():
            edges_arrived()

        @pl.when((t >= 2) & (t < 5))
        def _():
            convolve(t - 2)

        @pl.when(t == 5)
        def _():
            decode()

        settled = known - 1

        @pl.when(within(settled) & (role == 1))
        def _():
            for slot in range(3):
                arrived(slot, settled)

        rising = settled - HOP * z
        falling = settled - HOP * (rows - 1 - z)
        final = settled - HOP * (rows - 1)
        crossed = final - LAG
        ready = crossed - 1

        @pl.when(within(rising) & waves(rising))
        def _():
            @pl.when(z > 0)
            def _():
                wave(up_out, up_in, 4, rising, 4).wait_recv()

            @pl.when(z < rows - 1)
            def _():
                for part in range(2):
                    up_out[rising, part] = jnp.where(
                        group == z, mine(rising, part), up_in[rising, part]
                    )
                wave(up_out, up_in, 4, rising, 4).start()

        @pl.when(within(falling) & waves(falling))
        def _():
            @pl.when(z < rows - 1)
            def _():
                wave(down_out, down_in, 5, falling, -4).wait_recv()

            @pl.when(z > 0)
            def _():
                for part in range(2):
                    down_out[falling, part] = jnp.where(
                        group == z, mine(falling, part), down_in[falling, part]
                    )
                wave(down_out, down_in, 5, falling, -4).start()

        @pl.when(within(final) & waves(final))
        def _():
            for part in range(2):
                value = jnp.where(group < z, up_in[final, part], down_in[final, part])
                slots[3, final, part] = jnp.where(group == z, mine(final, part), value)

            @pl.when((role == 3) & crosses(final))
            def _():
                to_slot(slots.at[3, final], 3, final, 7, -2).start()

            @pl.when((role == 1) & crosses_back(final))
            def _():
                to_slot(slots.at[3, final], 3, final, 7, 2).start()

            to_slot(slots.at[3, final], 3, final, 6, -1).start()

        @pl.when(within(crossed))
        def _():
            @pl.when(((role == 1) & crosses(crossed)) | ((role == 3) & crosses_back(crossed)))
            def _():
                arrived(3, crossed)
                to_slot(slots.at[3, crossed], 3, crossed, 6, -1).start()

        @pl.when(pair_ends(settled))
        def _():
            attend_window((settled - 1, settled))

        @pl.when(pair_ends(ready))
        def _():
            @pl.when((role == 0) | (role == 2))
            def _():
                arrived(3, ready - 1)
                arrived(3, ready)

            attend_anchor((ready - 1, ready))

        return 0

    lax.fori_loop(0, PIECES + 2 * LAG + 2 + HOP * (rows - 1), step, 0)

    def finish(piece, _):
        for which in range(4):

            @pl.when(role == which)
            def _():
                for slot, lane, offset in direct[which]:
                    to_slot(own(piece), slot, piece, lane, offset).wait_send()
                for slot, there, lane, offset in passed.get(which, ()) + passed_again.get(which, ()):
                    to_slot(slots.at[slot, piece], there, piece, lane, offset).wait_send()

        @pl.when(waves(piece) & (z < rows - 1))
        def _():
            wave(up_out, up_in, 4, piece, 4).wait_send()

        @pl.when(waves(piece) & (z > 0))
        def _():
            wave(down_out, down_in, 5, piece, -4).wait_send()

        @pl.when((role == 1) | (role == 3))
        def _():
            to_slot(slots.at[3, piece], 3, piece, 6, -1).wait_send()

        @pl.when(((role == 3) & crosses(piece)) | ((role == 1) & crosses_back(piece)))
        def _():
            to_slot(slots.at[3, piece], 3, piece, 7, -3).wait_send()

        @pl.when(role == 2)
        def _():
            to_relay(piece, 4).wait_send()

        @pl.when(relayed(piece))
        def _():
            to_slot(relay.at[piece], 1, piece, 8, 4).wait_send()

        return 0

    lax.fori_loop(0, PIECES, finish, 0)

    @pl.when(me < n - 1)
    def _():
        edge(0).wait_send()

    @pl.when(me > 0)
    def _():
        edge(1).wait_send()


def shards(
    queries,
    keys_values,
    owner,
    span_mask,
    lengths,
    frames,
    past_frames,
    norm_gain,
    conv_weight,
    conv_bias,
):
    n = lax.axis_size("span")
    rows, cols = queries.shape
    piece = (PIECES, 2, rows, cols // PIECES)
    frame_count, _, frame_cols, channels = frames.shape
    padded = -(-(frame_cols + 1) // 16) * 16
    attention_flops = 4 * rows * 5 * rows * cols
    conv_flops = 2 * frame_count * frame_cols * conv_weight.size
    scalars = pl.BlockSpec(memory_space=pltpu.SMEM)
    whole = pl.BlockSpec(memory_space=pltpu.VMEM)
    return pl.pallas_call(
        functools.partial(block_kernel, n),
        out_shape=(
            jax.ShapeDtypeStruct((rows, cols), jnp.bfloat16),
            jax.ShapeDtypeStruct(frames.shape, jnp.bfloat16),
        ),
        in_specs=[scalars] * 3 + [whole] * 6 + [pl.BlockSpec(memory_space=pl.ANY)],
        out_specs=(whole, whole),
        scratch_shapes=[
            pltpu.VMEM((4,) + piece, jnp.bfloat16),
            pltpu.VMEM(piece, jnp.bfloat16),
            pltpu.VMEM((PIECES, rows, DH), jnp.float32),
            pltpu.VMEM((PIECES, rows, DH), jnp.float32),
            pltpu.VMEM((PIECES, rows, DH), jnp.float32),
            pltpu.VMEM(piece, jnp.bfloat16),
            pltpu.VMEM(piece, jnp.bfloat16),
            pltpu.VMEM(piece, jnp.bfloat16),
            pltpu.VMEM(piece, jnp.bfloat16),
            pltpu.VMEM((3, frame_count + past_frames.shape[0], padded, channels), jnp.bfloat16),
            pltpu.VMEM(conv_weight.shape, jnp.bfloat16),
            pltpu.VMEM((3, frame_count, padded + 16, channels), jnp.float32),
            pltpu.SemaphoreType.DMA((7, PIECES)),
            pltpu.SemaphoreType.DMA((9, PIECES)),
            pltpu.SemaphoreType.DMA((2,)),
            pltpu.SemaphoreType.DMA((2,)),
            pltpu.SemaphoreType.DMA,
        ],
        cost_estimate=pl.CostEstimate(
            flops=attention_flops + conv_flops,
            bytes_accessed=8 * rows * cols + 2 * conv_weight.size,
            transcendentals=5 * rows * rows * cols // DH,
        ),
        compiler_params=pltpu.CompilerParams(
            collective_id=0, has_side_effects=True, vmem_limit_bytes=60 * 1024 * 1024
        ),
        name="spans_and_decoder",
    )(
        owner,
        span_mask.T,
        lengths,
        queries,
        keys_values,
        frames,
        jnp.transpose(past_frames, (1, 2, 0, 3)),
        norm_gain,
        conv_bias,
        conv_weight,
    )


def solution(mesh):
    placed = (
        P(("group", "span"), None),
        P(None, ("group", "span"), None),
        P("group"),
        P("group", None),
        P("group"),
        P("group", "span", None, None),
        P("group", "span", None, None),
        P(),
        P(),
        P(),
    )
    return jax.shard_map(
        shards,
        mesh=mesh,
        in_specs=placed,
        out_specs=(P(("group", "span"), None), P("group", "span", None, None)),
        check_vma=False,
    )
```

```python
import functools

import jax
import jax.numpy as jnp
from jax import lax
from jax.experimental import pallas as pl
from jax.experimental.pallas import tpu as pltpu
from jax.sharding import PartitionSpec as P

DH = 128
WIN = 4
PIECES = 20
AHEAD = 4
HOP = 2
LAG = 2
LOG2E = 1.4426950408889634
MESH = pl.DeviceIdType.MESH


def block_kernel(
    n,
    owner_ref,
    mask_ref,
    lengths_ref,
    q_ref,
    kv_ref,
    frames_ref,
    past_ref,
    gain_ref,
    shift_ref,
    weight_ref,
    out_ref,
    decoded_ref,
    slots,
    relay,
    sums,
    tops,
    totals,
    up_in,
    down_in,
    up_out,
    down_out,
    taps,
    weights_here,
    partial,
    recv,
    send,
    edge_recv,
    edge_send,
    weight_sem,
):
    tokens = q_ref.shape[0]
    frames, _, cols, channels = frames_ref.shape
    past = past_ref.shape[2]
    padded = taps.shape[2]
    rows = n // 4
    width = q_ref.shape[1] // PIECES
    me = lax.axis_index("span")
    role = lax.rem(me, 4)
    z = me // 4

    def at(offset):
        return lax.rem(me + offset + n, n)

    def columns(piece):
        return pl.ds(pl.multiple_of(piece * width, width), width)

    def own(piece):
        return kv_ref.at[:, :, columns(piece)]

    def to_slot(source, slot, piece, lane, offset):
        return pltpu.make_async_remote_copy(
            src_ref=source,
            dst_ref=slots.at[slot, piece],
            send_sem=send.at[lane, piece],
            recv_sem=recv.at[slot, piece],
            device_id={"span": at(offset)},
            device_id_type=MESH,
        )

    def wave(source, target, kind, piece, offset):
        return pltpu.make_async_remote_copy(
            src_ref=source.at[piece],
            dst_ref=target.at[piece],
            send_sem=send.at[kind, piece],
            recv_sem=recv.at[kind, piece],
            device_id={"span": at(offset)},
            device_id_type=MESH,
        )

    def arrived(slot, piece):
        to_slot(slots.at[slot, piece], slot, piece, 0, 1).wait_recv()

    def edge(which):
        return pltpu.make_async_remote_copy(
            src_ref=taps.at[1],
            dst_ref=taps.at[2 * which],
            send_sem=edge_send.at[which],
            recv_sem=edge_recv.at[which],
            device_id={"span": at(1 - 2 * which)},
            device_id_type=MESH,
        )

    weight_copy = pltpu.make_async_copy(weight_ref, weights_here, weight_sem)
    weight_copy.start()

    barrier = pltpu.get_barrier_semaphore()
    for offset in (-4, -3, -2, -1, 1, 2, 3, 4):
        pl.semaphore_signal(barrier, inc=1, device_id={"span": at(offset)}, device_id_type=MESH)
    pl.semaphore_wait(barrier, 8)

    direct = {
        0: ((1, 1, 2), (0, 0, 1)),
        1: ((2, 0, 3), (1, 1, 2)),
        2: ((0, 0, 1),),
        3: ((2, 0, 3),),
    }

    def even(piece):
        return lax.rem(piece, 2) == 0

    def to_relay(piece, offset):
        return pltpu.make_async_remote_copy(
            src_ref=own(piece),
            dst_ref=relay.at[piece],
            send_sem=send.at[1, piece],
            recv_sem=recv.at[6, piece],
            device_id={"span": at(offset)},
            device_id_type=MESH,
        )

    def relayed(piece):
        return ((role == 0) & even(piece)) | ((role == 2) & jnp.logical_not(even(piece)))

    def pass_relayed(piece):
        @pl.when(relayed(piece))
        def _():
            to_relay(piece, 1).wait_recv()

        @pl.when((role == 0) & even(piece))
        def _():
            to_slot(relay.at[piece], 1, piece, 8, 4).start()

        @pl.when((role == 2) & jnp.logical_not(even(piece)))
        def _():
            to_slot(relay.at[piece], 1, piece, 8, -2).start()

    def send_own(piece):
        @pl.when((role == 2) & even(piece))
        def _():
            to_relay(piece, -2).start()

        @pl.when((role == 2) & jnp.logical_not(even(piece)))
        def _():
            to_relay(piece, 4).start()

        for which, copies in direct.items():

            @pl.when(role == which)
            def _():
                for slot, lane, offset in copies:
                    to_slot(own(piece), slot, piece, lane, offset).start()

    passed = {2: ((2, 0, 2, -2), (1, 2, 3, 1)), 3: ((1, 0, 2, -1),)}
    passed_again = {0: ((1, 2, 2, 1), (0, 1, 3, 1))}
    kept = {0: (2,), 2: (0,), 3: (0, 2)}

    def pass_on(piece, table):
        for which, copies in table.items():

            @pl.when(role == which)
            def _():
                for slot, there, lane, offset in copies:
                    arrived(slot, piece)
                    to_slot(slots.at[slot, piece], there, piece, lane, offset).start()

    def keep(piece):
        for which, slots_here in kept.items():

            @pl.when(role == which)
            def _():
                for slot in slots_here:
                    arrived(slot, piece)

    anchor = owner_ref[0]
    behind = lax.rem(me - anchor + n, n)
    group = jnp.where(role == 1, lax.rem((anchor + 2) // 4, rows), anchor // 4)

    def mine(piece, part):
        value = jnp.where(behind == 2, slots[1, piece, part], slots[2, piece, part])
        value = jnp.where(behind == 1, slots[0, piece, part], value)
        return jnp.where(behind == 0, kv_ref[part, :, columns(piece)], value)

    waves = lax.rem(role, 2) == 1

    def within(piece):
        return (piece >= 0) & (piece < PIECES)

    position = lax.rem(me - anchor - 1 + 2 * n, n)
    length = lengths_ref[me]
    limits = [length]
    for offset in range(1, WIN):
        allowed = (position >= offset) & (mask_ref[offset - 1, position] == 1)
        limits.append(jnp.where(allowed, lengths_ref[at(-offset)], 0))
    limits.append(jnp.where(behind == 0, 0, lengths_ref[anchor]))

    def activate():
        spare = partial.at[0, 0, 0:padded, :]
        for frame in range(past + frames):
            if frame < past:
                value = past_ref[0].astype(jnp.float32)[:, frame, :]
            else:
                value = frames_ref[frame - past, 0].astype(jnp.float32)
                squares = jnp.mean(value * value, axis=-1, keepdims=True)
                value = value * lax.rsqrt(squares + 1e-06) * gain_ref[...].reshape(1, channels)
                value = value / (1.0 + jnp.exp(-value))
            spare[...] = jnp.zeros(spare.shape, jnp.float32)
            spare[0:cols, :] = value
            taps[1, frame] = spare[...].astype(jnp.bfloat16)
        partial[0, :, 0:8, :] = jnp.zeros((frames, 8, channels), jnp.float32)

        @pl.when(me < n - 1)
        def _():
            edge(0).start()

        @pl.when(me > 0)
        def _():
            edge(1).start()

        @pl.when(me == 0)
        def _():
            taps[0] = jnp.zeros(taps.shape[1:], taps.dtype)

        @pl.when(me == n - 1)
        def _():
            taps[2] = jnp.zeros(taps.shape[1:], taps.dtype)

    def edges_arrived():
        @pl.when(me > 0)
        def _():
            edge(0).wait_recv()

        @pl.when(me < n - 1)
        def _():
            edge(1).wait_recv()

        weight_copy.wait()

    def convolve(col_tap):
        total = None
        for frame_tap in range(3):
            for row_tap in range(3):
                window_rows = taps[row_tap, frame_tap : frame_tap + frames]
                term = jnp.dot(
                    window_rows.reshape(frames * padded, channels),
                    weights_here[frame_tap, row_tap, col_tap],
                    preferred_element_type=jnp.float32,
                )
                total = term if total is None else total + term
        partial[col_tap, :, 8 : 8 + padded, :] = total.reshape(frames, padded, channels)

    def decode():
        for frame in range(frames):
            total = frames_ref[frame, 0].astype(jnp.float32) + shift_ref[...].reshape(1, channels)
            for col_tap in range(3):
                total = total + partial[col_tap, frame, 7 + col_tap : 7 + col_tap + cols, :]
            decoded_ref[frame, 0] = total.astype(decoded_ref.dtype)

    token = lax.broadcasted_iota(jnp.int32, (1, tokens), 1)
    row = lax.broadcasted_iota(jnp.int32, (tokens, 1), 0)

    def scores_of(piece, key, limit):
        score = lax.dot_general(
            q_ref[:, columns(piece)], key, (((1,), (1,)), ((), ())), preferred_element_type=jnp.float32
        )
        return score * (DH**-0.5 * LOG2E) + jnp.where(token < limit, 0.0, -1e30)

    def blend(weights, value):
        wide = jnp.concatenate([value, jnp.ones_like(value)], axis=1)
        return jnp.dot(weights.astype(jnp.bfloat16), wide, preferred_element_type=jnp.float32)

    def attend_window(pieces):
        scores = []
        for piece in pieces:
            keys = [kv_ref[0, :, columns(piece)]] + [slots[slot, piece, 0] for slot in range(WIN - 1)]
            scores.append([scores_of(piece, key, limit) for key, limit in zip(keys, limits)])
        for which, piece in enumerate(pieces):
            values = [kv_ref[1, :, columns(piece)]] + [slots[slot, piece, 1] for slot in range(WIN - 1)]
            top = jnp.max(functools.reduce(jnp.maximum, scores[which]), axis=-1, keepdims=True)
            blended = [
                blend(jnp.exp2(score - top), value) for score, value in zip(scores[which], values)
            ]
            blended = functools.reduce(jnp.add, blended)
            sums[piece] = blended[:, :DH]
            totals[piece] = blended[:, DH:]
            tops[piece] = jnp.broadcast_to(top, tops.shape[1:])

    def attend_anchor(pieces):
        scores = [scores_of(piece, slots[3, piece, 0], limits[WIN]) for piece in pieces]
        for score, piece in zip(scores, pieces):
            before = tops[piece]
            top = jnp.maximum(before, jnp.max(score, axis=-1, keepdims=True))
            added = blend(jnp.exp2(score - top[:, :1]), slots[3, piece, 1])
            scale = jnp.exp2(before - top)
            total = totals[piece] * scale + added[:, DH:]
            blended = (sums[piece] * scale + added[:, :DH]) / total
            out_ref[:, columns(piece)] = jnp.where(row < length, blended, 0.0).astype(out_ref.dtype)

    def pair_ends(piece):
        return within(piece) & (lax.rem(piece, 2) == 1)

    def start(piece, _):
        send_own(piece)
        return 0

    lax.fori_loop(0, AHEAD, start, 0)
    activate()

    def step(t, _):
        @pl.when(t + AHEAD < PIECES)
        def _():
            send_own(t + AHEAD)

        @pl.when(t < PIECES)
        def _():
            pass_on(t, passed)
            pass_relayed(t)

        known = t - LAG

        @pl.when(within(known))
        def _():
            pass_on(known, passed_again)
            keep(known)

        @pl.when(t == 2)
        def _():
            edges_arrived()

        @pl.when((t >= 2) & (t < 5))
        def _():
            convolve(t - 2)

        @pl.when(t == 5)
        def _():
            decode()

        settled = known - 1

        @pl.when(within(settled) & (role == 1))
        def _():
            for slot in range(3):
                arrived(slot, settled)

        rising = settled - HOP * z
        falling = settled - HOP * (rows - 1 - z)
        final = settled - HOP * (rows - 1)
        ready = final - 1

        @pl.when(within(rising) & waves)
        def _():
            @pl.when(z > 0)
            def _():
                wave(up_out, up_in, 4, rising, 4).wait_recv()

            @pl.when(z < rows - 1)
            def _():
                for part in range(2):
                    up_out[rising, part] = jnp.where(
                        group == z, mine(rising, part), up_in[rising, part]
                    )
                wave(up_out, up_in, 4, rising, 4).start()

        @pl.when(within(falling) & waves)
        def _():
            @pl.when(z < rows - 1)
            def _():
                wave(down_out, down_in, 5, falling, -4).wait_recv()

            @pl.when(z > 0)
            def _():
                for part in range(2):
                    down_out[falling, part] = jnp.where(
                        group == z, mine(falling, part), down_in[falling, part]
                    )
                wave(down_out, down_in, 5, falling, -4).start()

        @pl.when(within(final) & waves)
        def _():
            for part in range(2):
                value = jnp.where(group < z, up_in[final, part], down_in[final, part])
                slots[3, final, part] = jnp.where(group == z, mine(final, part), value)

            to_slot(slots.at[3, final], 3, final, 6, -1).start()

        @pl.when(pair_ends(settled))
        def _():
            attend_window((settled - 1, settled))

        @pl.when(pair_ends(ready))
        def _():
            @pl.when((role == 0) | (role == 2))
            def _():
                arrived(3, ready - 1)
                arrived(3, ready)

            attend_anchor((ready - 1, ready))

        return 0

    lax.fori_loop(0, PIECES + LAG + 2 + HOP * (rows - 1), step, 0)

    def finish(piece, _):
        for which in range(4):

            @pl.when(role == which)
            def _():
                for slot, lane, offset in direct[which]:
                    to_slot(own(piece), slot, piece, lane, offset).wait_send()
                for slot, there, lane, offset in passed.get(which, ()) + passed_again.get(which, ()):
                    to_slot(slots.at[slot, piece], there, piece, lane, offset).wait_send()

        @pl.when(waves & (z < rows - 1))
        def _():
            wave(up_out, up_in, 4, piece, 4).wait_send()

        @pl.when(waves & (z > 0))
        def _():
            wave(down_out, down_in, 5, piece, -4).wait_send()

        @pl.when((role == 1) | (role == 3))
        def _():
            to_slot(slots.at[3, piece], 3, piece, 6, -1).wait_send()

        @pl.when(role == 2)
        def _():
            to_relay(piece, 4).wait_send()

        @pl.when(relayed(piece))
        def _():
            to_slot(relay.at[piece], 1, piece, 8, 4).wait_send()

        return 0

    lax.fori_loop(0, PIECES, finish, 0)

    @pl.when(me < n - 1)
    def _():
        edge(0).wait_send()

    @pl.when(me > 0)
    def _():
        edge(1).wait_send()


def shards(
    queries,
    keys_values,
    owner,
    span_mask,
    lengths,
    frames,
    past_frames,
    norm_gain,
    conv_weight,
    conv_bias,
):
    n = lax.axis_size("span")
    rows, cols = queries.shape
    piece = (PIECES, 2, rows, cols // PIECES)
    frame_count, _, frame_cols, channels = frames.shape
    padded = -(-(frame_cols + 1) // 16) * 16
    attention_flops = 4 * rows * 5 * rows * cols
    conv_flops = 2 * frame_count * frame_cols * conv_weight.size
    scalars = pl.BlockSpec(memory_space=pltpu.SMEM)
    whole = pl.BlockSpec(memory_space=pltpu.VMEM)
    return pl.pallas_call(
        functools.partial(block_kernel, n),
        out_shape=(
            jax.ShapeDtypeStruct((rows, cols), jnp.bfloat16),
            jax.ShapeDtypeStruct(frames.shape, jnp.bfloat16),
        ),
        in_specs=[scalars] * 3 + [whole] * 6 + [pl.BlockSpec(memory_space=pl.ANY)],
        out_specs=(whole, whole),
        scratch_shapes=[
            pltpu.VMEM((4,) + piece, jnp.bfloat16),
            pltpu.VMEM(piece, jnp.bfloat16),
            pltpu.VMEM((PIECES, rows, DH), jnp.float32),
            pltpu.VMEM((PIECES, rows, DH), jnp.float32),
            pltpu.VMEM((PIECES, rows, DH), jnp.float32),
            pltpu.VMEM(piece, jnp.bfloat16),
            pltpu.VMEM(piece, jnp.bfloat16),
            pltpu.VMEM(piece, jnp.bfloat16),
            pltpu.VMEM(piece, jnp.bfloat16),
            pltpu.VMEM((3, frame_count + past_frames.shape[0], padded, channels), jnp.bfloat16),
            pltpu.VMEM(conv_weight.shape, jnp.bfloat16),
            pltpu.VMEM((3, frame_count, padded + 16, channels), jnp.float32),
            pltpu.SemaphoreType.DMA((7, PIECES)),
            pltpu.SemaphoreType.DMA((9, PIECES)),
            pltpu.SemaphoreType.DMA((2,)),
            pltpu.SemaphoreType.DMA((2,)),
            pltpu.SemaphoreType.DMA,
        ],
        cost_estimate=pl.CostEstimate(
            flops=attention_flops + conv_flops,
            bytes_accessed=8 * rows * cols + 2 * conv_weight.size,
            transcendentals=5 * rows * rows * cols // DH,
        ),
        compiler_params=pltpu.CompilerParams(
            collective_id=0, has_side_effects=True, vmem_limit_bytes=60 * 1024 * 1024
        ),
        name="spans_and_decoder",
    )(
        owner,
        span_mask.T,
        lengths,
        queries,
        keys_values,
        frames,
        jnp.transpose(past_frames, (1, 2, 0, 3)),
        norm_gain,
        conv_bias,
        conv_weight,
    )


def solution(mesh):
    placed = (
        P(("group", "span"), None),
        P(None, ("group", "span"), None),
        P("group"),
        P("group", None),
        P("group"),
        P("group", "span", None, None),
        P("group", "span", None, None),
        P(),
        P(),
        P(),
    )
    return jax.shard_map(
        shards,
        mesh=mesh,
        in_specs=placed,
        out_specs=(P(("group", "span"), None), P("group", "span", None, None)),
        check_vma=False,
    )
```
